512 devices in a mesh: members: 8 (over y), bands: 64 (over z, x, core).
Axes of the slice: x: 4, y: 8, z: 8, core: 2. Of those that a mesh axis runs over, the one named last changes fastest.
Arguments:
- ensemble: float32 [128, 1024, 128], P('members', 'bands'), may hold values from -6 to 6
- neighbours: int32 [1024, 4], P('bands'), may hold values from 0 to 1023, as said below
- regime: int32 [1024], P('bands'), may hold values from 0 to 3
- norm_gain: float32 [128], replicated, may hold values from 0.25 to 1.75
- up_weight: bfloat16 [4, 128, 512], replicated, may hold values from -0.5 to 0.5
- down_weight: bfloat16 [4, 512, 128], replicated, may hold values from -0.25 to 0.25
- vertical_modes: float32 [4, 128], replicated, may hold values from -3 to 3
- obs_col: int32 [16384], P('bands'), may hold values from 0 to 1023, as said below
- obs_lev: int32 [16384], P('bands'), may hold values from 0 to 127
- obs_val: float32 [16384], P('bands'), may hold values from -9 to 9
- obs_err: float32 [16384], P('bands'), may hold values from 0.3 to 1
Outputs:
- analysis: float32 [128, 1024, 128], P('members', 'bands')
The draws below stay inside these ranges and needn't reach their ends.
Inputs may be any that keep to these rules, and one draw needn't show every extreme that they name: `neighbours`: every neighbour of column c lies within 8 columns of c. `obs_col`: the observations at positions b * 256 to (b + 1) * 256 - 1 lie in columns b * 16 to (b + 1) * 16 - 1.
All inputs are finite; a program needn't handle non-finite values.
Results may differ from the reference program's by a relative error of at most 0.0034.
Values sent between devices are 32-bit elements; how exact they have to be, the bound alone decides.
No kernel may reach another device: no remote copies, remote signals or barrier semaphores. Data moves between devices by JAX's collectives and lax.ppermute only.
A program may use at most 64 MiB of HBM per device.

```python
import math
from functools import partial
import jax
import jax.numpy as jnp
from jax import lax

M = 128
LEV = 128
FF = 512
E = 4
L = 4
NB = 4
HALO = 8
NS_ITERS = 4
C_DEV = 16
OBS_DEV = 256
EXPANDED_SIZE = 512
COLS = 1024
NOBS = 16384


def draw_neighbours(key, part):
    first_key, second_key = jax.random.split(jax.random.fold_in(key, 11))
    column = jnp.arange(COLS, dtype=jnp.int32)[:, None]
    offsets = jax.random.randint(first_key, (COLS, NB), -HALO, HALO + 1)
    signs = 2 * jax.random.randint(second_key, (COLS, 1), 0, 2) - 1
    offsets = jnp.concatenate([signs * HALO, offsets[:, 1:]], axis=1)
    return jnp.clip(column + offsets, 0, COLS - 1).astype(jnp.int32)


def draw_obs_col(key, part):
    band_of = jnp.arange(NOBS, dtype=jnp.int32) // OBS_DEV
    inside = jax.random.randint(jax.random.fold_in(key, 23), (NOBS,), 0, C_DEV)
    return (band_of * C_DEV + inside).astype(jnp.int32)


def touch_ends(entries, rng, least, high):
    extent = entries.shape
    place = [jax.random.randint(jax.random.fold_in(rng, axis), (), 0, extent[axis]) for axis in range(len(extent))]
    entries = entries.at[tuple(place)].set(least)
    longest = extent.index(max(extent))
    place[longest] = (place[longest] + 1) % extent[longest]
    return entries.at[tuple(place)].set(high)


def shard_levels(rng, dims, cuts, smallest, top_value):
    def one(dim, shards_of):
        heights = jax.random.uniform(jax.random.fold_in(jax.random.fold_in(rng, 6), dim), (shards_of,), jnp.float32, smallest / len(cuts), top_value / len(cuts))
        return jnp.repeat(jnp.exp(heights), dims[dim] // shards_of).reshape((-1,) + (1,) * (len(dims) - dim - 1))

    level = one(*cuts[0])
    for cut in cuts[1:]:
        level = level * one(*cut)
    return level


def bell_draw(own_key, extent, scale, most, shards=(), held_as=jnp.bfloat16):
    drawn = scale * jax.random.normal(own_key, extent, jnp.float32)
    if shards:
        drawn = drawn * shard_levels(own_key, extent, shards, -0.22, 0.18)
    return jnp.clip(drawn, -most, most).astype(held_as)


def setup_inputs(seed: int = 0) -> dict:
    key_list = jax.random.split(jax.random.key(seed), 12)
    return {
        "ensemble": bell_draw(key_list[0], (M, COLS, LEV), 1.0, 6.0, ((0, 8), (1, 64)), jnp.float32),
        "neighbours": draw_neighbours(jax.random.fold_in(key_list[11], 71), 0),
        "regime": touch_ends(jax.random.randint(key_list[2], (COLS,), 0, E), jax.random.fold_in(key_list[2], 1), 0, E - 1).astype(jnp.int32),
        "norm_gain": jnp.clip(1.0 + 0.15 * jax.random.normal(key_list[3], (LEV,), jnp.float32), 0.25, 1.75),
        "up_weight": bell_draw(key_list[4], (E, LEV, FF), LEV ** -0.5, 0.5),
        "down_weight": bell_draw(key_list[5], (E, FF, LEV), FF ** -0.5, 0.25),
        "vertical_modes": bell_draw(key_list[6], (L, LEV), 1.0, 3.0, (), jnp.float32),
        "obs_col": draw_obs_col(jax.random.fold_in(key_list[11], 71), 0),
        "obs_lev": touch_ends(jax.random.randint(key_list[8], (NOBS,), 0, LEV), jax.random.fold_in(key_list[8], 1), 0, LEV - 1).astype(jnp.int32),
        "obs_val": bell_draw(key_list[9], (NOBS,), 3.0, 9.0, ((0, 64),), jnp.float32),
        "obs_err": jnp.clip(jnp.exp(math.log(1.0) - 1.2039728 * jax.random.uniform(key_list[10], (NOBS,), jnp.float32) ** shard_levels(key_list[10], (NOBS,), ((0, 64),), -0.2, 0.2)), 0.3, 1.0),
    }


highest = lax.Precision.HIGHEST

def expert_block(item, norm_gain, up_weight, down_weight):
    block_state, block_regime = item
    members_here, width_cols, level_count = block_state.shape
    flat = block_state.reshape(members_here * width_cols, level_count)
    inv_rms = lax.rsqrt(lax.optimization_barrier(jnp.mean(flat * flat, axis=1, keepdims=True)) + 1e-05)
    normed = (flat * inv_rms * norm_gain).astype(jnp.bfloat16)
    result = jnp.zeros(flat.shape, jnp.float32)
    for expert in range(E):
        hits = jnp.tile(block_regime == expert, members_here)

        def active(values, expert=expert):
            hidden = jax.nn.silu(jnp.dot(values, up_weight[expert], preferred_element_type=jnp.float32)).astype(jnp.bfloat16)
            return jnp.dot(hidden, down_weight[expert], preferred_element_type=jnp.float32)

        def absent(values):
            return jnp.zeros((values.shape[0], level_count), jnp.float32)
        output = lax.cond(jnp.any(hits), active, absent, normed)
        result = result + jnp.where(hits[:, None], output, 0.0)
    return result.reshape(members_here, width_cols, level_count)

def analysis_coefficients(gram_matrix, cross_terms, drive_terms):
    order_k = gram_matrix.shape[0]
    identity = jnp.eye(order_k, dtype=jnp.float32)
    system = identity + gram_matrix
    norm_scale = jnp.sqrt(jnp.sum(system * system))
    iterate = system / norm_scale
    inverse = identity
    for sweep_index in range(NS_ITERS):
        if sweep_index == 0:
            product = iterate
        else:
            product = jnp.dot(inverse, iterate, precision=highest)
        factor = 1.5 * identity - 0.5 * product
        if sweep_index + 1 < NS_ITERS:
            iterate = jnp.dot(iterate, factor, precision=highest)
        if sweep_index == 0:
            inverse = factor
        else:
            inverse = jnp.dot(factor, inverse, precision=highest)
    root_factor = inverse / jnp.sqrt(norm_scale)
    weights_matrix = jnp.dot(root_factor, root_factor, precision=highest)
    mean_weights = jnp.dot(weights_matrix, drive_terms, precision=highest)
    return mean_weights[:, None] - 0.5 * jnp.dot(weights_matrix, cross_terms, precision=highest)

def reference(ensemble, neighbours, regime, norm_gain, up_weight, down_weight, vertical_modes, obs_col, obs_lev, obs_val, obs_err):
    summed_nb = jnp.zeros_like(ensemble)
    for which in range(NB):
        summed_nb = summed_nb + ensemble[:, neighbours[:, which], :]
    filtered_profile = ensemble + 0.5 * (0.25 * summed_nb - ensemble)
    order = jnp.argsort(regime, stable=True).astype(jnp.int32)
    count_blocks = COLS // 8
    blocks = filtered_profile[:, order, :].reshape(M, count_blocks, 8, LEV).transpose(1, 0, 2, 3)
    block_regimes = regime[order].reshape(count_blocks, 8)
    outputs = lax.map(partial(expert_block, norm_gain=norm_gain, up_weight=up_weight, down_weight=down_weight), (blocks, block_regimes))
    tendency_sorted = outputs.transpose(1, 0, 2, 3).reshape(M, COLS, LEV)
    time_derivative = jnp.zeros_like(filtered_profile).at[:, order, :].set(tendency_sorted)
    predicted_vector = filtered_profile + time_derivative
    average_sample_vector = lax.optimization_barrier(jnp.mean(predicted_vector, axis=0))
    sample_anomaly = predicted_vector - average_sample_vector
    obs_pert = (sample_anomaly[:, obs_col, obs_lev] / obs_err).T
    innovation = (obs_val - average_sample_vector[obs_col, obs_lev]) / obs_err
    modulated = (vertical_modes[:, obs_lev].T[:, :, None] * obs_pert[:, None, :]).reshape(NOBS, EXPANDED_SIZE) / math.sqrt(EXPANDED_SIZE - 1)
    gram_matrix = jnp.dot(modulated.T, modulated, precision=highest)
    cross_terms = jnp.dot(modulated.T, obs_pert, precision=highest)
    drive_terms = jnp.dot(modulated.T, innovation, precision=highest)
    coefficients = analysis_coefficients(gram_matrix, cross_terms, drive_terms)
    coeff_modes = coefficients.reshape(L, M, M)
    update_correction = jnp.zeros_like(predicted_vector)
    for layer in range(L):
        mixed = jnp.einsum('acv,ab->bcv', sample_anomaly, coeff_modes[layer], precision=highest)
        update_correction = update_correction + vertical_modes[layer][None, None, :] * mixed
    return predicted_vector + update_correction / math.sqrt(EXPANDED_SIZE - 1)
```

```python
import functools
import math

import jax
import jax.numpy as jnp
from jax import lax
from jax.experimental import pallas as pl
from jax.experimental.pallas import tpu as pltpu
from jax.sharding import Mesh, PartitionSpec as P

E = 4
L = 4
NB = 4
HALO = 8
M = 128
LEV = 128
FF = 512
C = 16
MD = 16
OBS = 256
GROUPS = 8
PACKS = 7
PAIRS = [(a, b) for a in range(L) for b in range(a, L)]
ROOT = math.sqrt(L * M - 1)
BF = jnp.bfloat16
F32 = jnp.float32
VMEM_LIMIT = 48 * 1024 * 1024
BANDS = ("z", "x", "core")


def dot(a, b):
    return jnp.dot(a, b, preferred_element_type=F32)


def dot_nt(a, b):
    return lax.dot_general(a, b, (((1,), (1,)), ((), ())), preferred_element_type=F32)


def split2(a):
    high = a.astype(BF)
    return high, (a - high.astype(F32)).astype(BF)


def split3(a):
    high = a.astype(BF)
    rest = a - high.astype(F32)
    middle = rest.astype(BF)
    return high, middle, (rest - middle.astype(F32)).astype(BF)


def forecast_kernel(
    nb, regime, ens, low, high, gain, up, down, lev, col, err, modes,
    f_out, v_out, w_out, wide, regs,
):
    band = (lax.axis_index("z") * 4 + lax.axis_index("x")) * 2 + lax.axis_index("core")
    for c in range(C):
        wide[HALO + c] = ens[:, c, :]
        regs[c * MD:(c + 1) * MD, :] = jnp.full((MD, LEV), regime[c], jnp.int32)
    for c in range(HALO):
        wide[c] = low[:, c, :]
        wide[HALO + C + c] = high[:, c, :]
    start = band * C - HALO
    rows = []
    for c in range(C):
        total = wide[nb[c, 0] - start]
        for k in range(1, NB):
            total = total + wide[nb[c, k] - start]
        own = wide[HALO + c]
        rows.append(own + 0.5 * (0.25 * total - own))
    flat = jnp.concatenate(rows, axis=0)
    inv_rms = lax.rsqrt(jnp.mean(flat * flat, axis=1, keepdims=True) + 1e-05)
    normed = (flat * inv_rms * gain[...]).astype(BF)
    which = regs[...]
    which4 = jnp.concatenate([which] * (FF // LEV), axis=1)
    pre = dot(normed, up[0])
    for e in range(1, E):
        pre = jnp.where(which4 == e, dot(normed, up[e]), pre)
    hidden = pre / (1.0 + jnp.exp(-pre))
    out = flat
    tendency = None
    for e in range(E):
        part = dot(jnp.where(which4 == e, hidden, 0.0).astype(BF), down[e])
        tendency = part if tendency is None else tendency + part
    out = flat + tendency
    f_out[...] = out.reshape(C, MD, LEV)

    one_hot = (lax.broadcasted_iota(jnp.int32, (LEV, OBS), 0) == lev[...]).astype(F32).astype(BF)
    picked = None
    for part in split3(out):
        got = dot(part, one_hot)
        picked = got if picked is None else picked + got
    place = col[...] - band * C
    sampled = jnp.zeros((MD, OBS), F32)
    for c in range(C):
        sampled = sampled + jnp.where(place == c, picked[c * MD:(c + 1) * MD, :], 0.0)
    sampled = sampled / err[...]
    for g in range(GROUPS):
        v_out[g] = sampled
    at_obs = None
    for part in split3(modes[...]):
        got = dot(part, one_hot)
        at_obs = got if at_obs is None else at_obs + got
    w_out[...] = at_obs


def gram_kernel(values, at_obs, val, err, packed, centred):
    group = lax.axis_index("members")
    raw = values[...].reshape(M, OBS)
    mean = jnp.sum(raw, axis=0, keepdims=True) * (1.0 / M)
    pert = raw - mean
    again = jnp.sum(pert, axis=0, keepdims=True) * (1.0 / M)
    pert = pert - again
    centred[...] = pert
    innovation = val[...] / err[...] - (mean + again)
    own = centred[pl.ds(pl.multiple_of(group * MD, MD), MD), :]
    w = at_obs[...]
    weights = [w[a:a + 1] * w[b:b + 1] * (1.0 / (L * M - 1)) for a, b in PAIRS]
    weights += [w[a:a + 1] * (1.0 / ROOT) for a in range(L)]
    left = jnp.concatenate([own * f for f in weights], axis=0)
    right = jnp.concatenate(
        [pert, jnp.broadcast_to(innovation, (M, OBS))], axis=0
    )
    lh, ll = split2(left)
    rh, rl = split2(right)
    s = dot_nt(lh, rh) + (dot_nt(lh, rl) + dot_nt(ll, rh))
    row = lax.broadcasted_iota(jnp.int32, (MD, M), 0) + group * MD
    column = lax.broadcasted_iota(jnp.int32, (MD, M), 1)
    for t in range(PACKS):
        first = s[(2 * t) * MD:(2 * t + 1) * MD, :M]
        second = s[(2 * t + 1) * MD:(2 * t + 2) * MD, :M]
        if t < L:
            k = len(PAIRS) + t
            middle = s[k * MD:(k + 1) * MD, M:]
        else:
            middle = jnp.zeros((MD, M), F32)
        p = jnp.where(column > row, first, jnp.where(column < row, second, middle))
        for h in range(2):
            for x in range(4):
                packed[2 * x + h, t] = p[8 * h:8 * h + 8]


def analysis_kernel(
    mine, other, forecasts, own_forecast, modes, out,
    packed, crosses, zf, zh, zl, fh, fl,
):
    group = lax.axis_index("members")
    core = lax.axis_index("core")
    for g in range(GROUPS):
        for t in range(PACKS):
            at = pl.multiple_of(g * MD + core * 8, 8)
            packed[t, pl.ds(at, 8), :] = mine[g, t]
            at = pl.multiple_of(g * MD + 8 - core * 8, 8)
            packed[t, pl.ds(at, 8), :] = other[g, t]
    i = lax.broadcasted_iota(jnp.int32, (M, M), 0)
    j = lax.broadcasted_iota(jnp.int32, (M, M), 1)
    diagonal = i == j
    drives = []
    square = None
    for t in range(PACKS):
        p = packed[t]
        q = p.T
        if t < L:
            drives.append(jnp.sum(jnp.where(diagonal, p, 0.0), axis=0, keepdims=True))
        for side in range(2):
            keep = (i < j) if side == 0 else (i > j)
            s = jnp.where(diagonal, 0.0, jnp.where(keep, p, q))
            s = s - jnp.where(diagonal, jnp.sum(s, axis=0, keepdims=True), 0.0)
            k = 2 * t + side
            if k >= len(PAIRS):
                crosses[k - len(PAIRS)] = s
                continue
            a, b = PAIRS[k]
            if a == b:
                s = s + jnp.where(diagonal, 1.0, 0.0)
            zf[a * M:(a + 1) * M, b * M:(b + 1) * M] = s
            if a != b:
                zf[b * M:(b + 1) * M, a * M:(a + 1) * M] = s
            part = jnp.sum(s * s, axis=0, keepdims=True) * (1.0 if a == b else 2.0)
            square = part if square is None else square + part
    norm = jnp.sqrt(jnp.sum(square, axis=1, keepdims=True))
    inverse_norm = 1.0 / norm
    own_rows = pl.ds(pl.multiple_of(group * MD, MD), MD)
    v = jnp.concatenate(
        [drives[a] - 0.5 * crosses[a, own_rows, :] for a in range(L)], axis=1
    )
    z = zf[...] * inverse_norm
    size = L * M
    for step in range(3):
        high, low = split2(z)
        zf[...] = z
        zh[0:size] = high
        zl[0:size] = low
        vh, vl = split2(v)
        zh[size:size + MD] = vh
        zl[size:size + MD] = vl
        a, b = zh[0:size], zl[0:size]
        q = dot(a, a) + (dot(a, b) + dot(b, a))
        identity = (
            lax.broadcasted_iota(jnp.int32, (size, size), 0)
            == lax.broadcasted_iota(jnp.int32, (size, size), 1)
        )
        f = jnp.where(identity, 2.25, 0.0) - 1.5 * zf[...] + 0.25 * q
        high, low = split2(f)
        fh[...] = high
        fl[...] = low
        a, b = zh[...], zl[...]
        new = dot(a, fh[...]) + (dot(a, fl[...]) + dot(b, fh[...]))
        z = new[0:size]
        v = new[size:size + MD]
    high, low = split2(z)
    fh[...] = high
    fl[...] = low
    for step in range(2):
        vh, vl = split2(v)
        v = 1.5 * v - 0.5 * (dot(vh, fh[...]) + (dot(vh, fl[...]) + dot(vl, fh[...])))
    v = v * inverse_norm
    blocks = []
    for a in range(L):
        block = v[:, a * M:(a + 1) * M]
        blocks.append(block - jnp.mean(block, axis=1, keepdims=True))
    coeff = jnp.concatenate(blocks, axis=0)
    ch, cl = split2(coeff)
    both = jnp.concatenate([ch, cl], axis=0)
    scaled = modes[...] * (1.0 / ROOT)
    for c in range(0, C, 2):
        block = jnp.concatenate(
            [forecasts[:, c + k].reshape(M, LEV) for k in range(2)], axis=1
        )
        bh, bl = split2(block)
        r = dot(both, bh)
        r = r[:L * MD] + (r[L * MD:] + dot(ch, bl))
        for k in range(2):
            total = own_forecast[c + k]
            for a in range(L):
                total = total + scaled[a:a + 1] * r[a * MD:(a + 1) * MD, k * LEV:(k + 1) * LEV]
            out[:, c + k, :] = total


def call(kernel, outs, scratch, smem=0, total=0, name=None, flops=0):
    specs = [
        pl.BlockSpec(memory_space=pltpu.SMEM if n < smem else pltpu.VMEM)
        for n in range(total)
    ]
    return pl.pallas_call(
        kernel,
        out_shape=outs,
        in_specs=specs,
        out_specs=jax.tree.map(lambda _: pl.BlockSpec(memory_space=pltpu.VMEM), outs),
        scratch_shapes=scratch,
        compiler_params=pltpu.CompilerParams(vmem_limit_bytes=VMEM_LIMIT),
        name=name,
    )


def swap(x, axes):
    return lax.all_to_all(x, axes, split_axis=0, concat_axis=0, tiled=True)


def summed_copies(x, copies):
    total = jnp.sum(x, axis=0)
    return jnp.broadcast_to(total[None], (copies,) + total.shape)


def per_device(
    ensemble, neighbours, regime, norm_gain, up_weight, down_weight, vertical_modes,
    obs_col, obs_lev, obs_val, obs_err,
):
    shape = jax.ShapeDtypeStruct
    forward = [(n, n + 1) for n in range(63)]
    backward = [(b, a) for a, b in forward]
    low = lax.ppermute(ensemble[:, C - HALO:, :], BANDS, forward)
    high = lax.ppermute(ensemble[:, :HALO, :], BANDS, backward)
    lev = obs_lev.reshape(1, OBS)
    col = obs_col.reshape(1, OBS)
    val = obs_val.reshape(1, OBS)
    err = obs_err.reshape(1, OBS)
    forecast, values, at_obs = call(
        forecast_kernel,
        [shape((C, MD, LEV), F32), shape((GROUPS, MD, OBS), F32), shape((L, OBS), F32)],
        [pltpu.VMEM((C + 2 * HALO, MD, LEV), F32), pltpu.VMEM((C * MD, LEV), jnp.int32)],
        smem=2, total=12, name="forecast",
    )(
        neighbours, regime, ensemble, low, high, norm_gain.reshape(1, LEV), up_weight, down_weight,
        lev, col, err, vertical_modes,
    )
    values = swap(values, "members")
    gathered = lax.all_gather(forecast, "members")
    packed = call(
        gram_kernel,
        shape((8, PACKS, 8, M), F32),
        [pltpu.VMEM((M, OBS), F32)],
        total=4, name="gram",
    )(values, at_obs, val, err)
    packed = swap(packed, ("x", "core"))
    packed = swap(summed_copies(packed, 8), "z")
    mine = swap(summed_copies(packed, GROUPS), "members")
    other = lax.ppermute(mine, "core", [(0, 1), (1, 0)])
    size = L * M
    return call(
        analysis_kernel,
        shape((MD, C, LEV), F32),
        [
            pltpu.VMEM((PACKS, M, M), F32),
            pltpu.VMEM((L, M, M), F32),
            pltpu.VMEM((size, size), F32),
            pltpu.VMEM((size + MD, size), BF),
            pltpu.VMEM((size + MD, size), BF),
            pltpu.VMEM((size, size), BF),
            pltpu.VMEM((size, size), BF),
        ],
        total=5, name="analysis",
    )(mine, other, gathered, forecast, vertical_modes)


def solution(mesh):
    fine = Mesh(mesh.devices.reshape(8, 8, 4, 2), ("members",) + BANDS)
    in_specs = (
        P("members", BANDS, None),
        P(BANDS, None),
        P(BANDS),
        P(),
        P(),
        P(),
        P(),
        P(BANDS),
        P(BANDS),
        P(BANDS),
        P(BANDS),
    )
    out_specs = P("members", BANDS, None)
    return jax.shard_map(
        per_device, mesh=fine, in_specs=in_specs, out_specs=out_specs, check_vma=False
    )
```

```python
import functools
import math

import jax
import jax.numpy as jnp
from jax import lax
from jax.experimental import pallas as pl
from jax.experimental.pallas import tpu as pltpu
from jax.sharding import Mesh, PartitionSpec as P

E = 4
L = 4
NB = 4
HALO = 8
M = 128
LEV = 128
FF = 512
C = 16
MD = 16
OBS = 256
GROUPS = 8
PACKS = 7
PAIRS = [(a, b) for a in range(L) for b in range(a, L)]
ROOT = math.sqrt(L * M - 1)
BF = jnp.bfloat16
F32 = jnp.float32
VMEM_LIMIT = 40 * 1024 * 1024
FULL_LIMIT = 53 * 1024 * 1024
BANDS = ("z", "x", "core")


def dot(a, b):
    return jnp.dot(a, b, preferred_element_type=F32)


def dot_nt(a, b):
    return lax.dot_general(a, b, (((1,), (1,)), ((), ())), preferred_element_type=F32)


def split2(a):
    high = a.astype(BF)
    return high, (a - high.astype(F32)).astype(BF)


def split3(a):
    high = a.astype(BF)
    rest = a - high.astype(F32)
    middle = rest.astype(BF)
    return high, middle, (rest - middle.astype(F32)).astype(BF)


def prepare_kernel(
    regime, ens, up, down, col, lev, val, err, modes, gain,
    own_out, up_out, down_out, hot_out, regs_out, w_out, place_out,
):
    band = (lax.axis_index("z") * 4 + lax.axis_index("x")) * 2 + lax.axis_index("core")
    place_out[...] = col[...] - band * C
    for c in range(C):
        own_out[c] = ens[:, c, :]
        regs_out[c * MD:(c + 1) * MD, :] = jnp.full((MD, LEV), regime[c], jnp.int32)
    up_out[...] = up[...]
    down_out[...] = down[...]
    one_hot = (lax.broadcasted_iota(jnp.int32, (LEV, OBS), 0) == lev[...]).astype(F32).astype(BF)
    hot_out[...] = one_hot
    at_obs = None
    for part in split3(modes[...]):
        got = dot(part, one_hot)
        at_obs = got if at_obs is None else at_obs + got
    w_out[0:L, :] = at_obs
    w_out[L:L + 1, :] = val[...] / err[...]
    w_out[L + 1:L + 2, :] = err[...]
    w_out[L + 2:L + 3, 0:LEV] = gain[...]


def forecast_kernel(
    nb, own_columns, low, high, up, down, one_hot, which_ref, rows_in, place_in,
    f_out, v_out, wide,
):
    band = (lax.axis_index("z") * 4 + lax.axis_index("x")) * 2 + lax.axis_index("core")
    wide[HALO:HALO + C] = own_columns[...]
    for c in range(HALO):
        wide[c] = low[:, c, :]
        wide[HALO + C + c] = high[:, c, :]
    start = band * C - HALO
    rows = []
    for c in range(C):
        total = wide[nb[c, 0] - start]
        for k in range(1, NB):
            total = total + wide[nb[c, k] - start]
        own = own_columns[c]
        rows.append(own + 0.5 * (0.25 * total - own))
    flat = jnp.concatenate(rows, axis=0)
    inv_rms = lax.rsqrt(jnp.mean(flat * flat, axis=1, keepdims=True) + 1e-05)
    normed = (flat * inv_rms * rows_in[L + 2:L + 3, 0:LEV]).astype(BF)
    which = which_ref[...]
    which4 = jnp.concatenate([which] * (FF // LEV), axis=1)
    pre = dot(normed, up[0])
    for e in range(1, E):
        pre = jnp.where(which4 == e, dot(normed, up[e]), pre)
    hidden = pre / (1.0 + jnp.exp(-pre))
    tendency = None
    for e in range(E):
        part = dot(jnp.where(which4 == e, hidden, 0.0).astype(BF), down[e])
        tendency = part if tendency is None else tendency + part
    out = flat + tendency
    f_out[...] = out.reshape(C, MD, LEV)

    picked = None
    for part in split3(out):
        got = dot(part, one_hot[...])
        picked = got if picked is None else picked + got
    place = place_in[...]
    sampled = jnp.zeros((MD, OBS), F32)
    for c in range(C):
        sampled = sampled + jnp.where(place == c, picked[c * MD:(c + 1) * MD, :], 0.0)
    sampled = sampled / rows_in[L + 1:L + 2, :]
    for g in range(GROUPS):
        v_out[g] = sampled


def gram_kernel(values, at_obs, packed, centred):
    group = lax.axis_index("members")
    raw = values[...].reshape(M, OBS)
    mean = jnp.sum(raw, axis=0, keepdims=True) * (1.0 / M)
    pert = raw - mean
    again = jnp.sum(pert, axis=0, keepdims=True) * (1.0 / M)
    pert = pert - again
    centred[...] = pert
    innovation = at_obs[L:L + 1, :] - (mean + again)
    own = centred[pl.ds(pl.multiple_of(group * MD, MD), MD), :]
    w = at_obs[...]
    weights = [w[a:a + 1] * w[b:b + 1] * (1.0 / (L * M - 1)) for a, b in PAIRS]
    weights += [w[a:a + 1] * (1.0 / ROOT) for a in range(L)]
    left = jnp.concatenate([own * f for f in weights], axis=0)
    right = jnp.concatenate(
        [pert, jnp.broadcast_to(innovation, (M, OBS))], axis=0
    )
    lh, ll = split2(left)
    rh, rl = split2(right)
    s = dot_nt(lh, rh) + (dot_nt(lh, rl) + dot_nt(ll, rh))
    row = lax.broadcasted_iota(jnp.int32, (MD, M), 0) + group * MD
    column = lax.broadcasted_iota(jnp.int32, (MD, M), 1)
    for t in range(PACKS):
        first = s[(2 * t) * MD:(2 * t + 1) * MD, :M]
        second = s[(2 * t + 1) * MD:(2 * t + 2) * MD, :M]
        if t < L:
            k = len(PAIRS) + t
            middle = s[k * MD:(k + 1) * MD, M:]
        else:
            middle = jnp.zeros((MD, M), F32)
        p = jnp.where(column > row, first, jnp.where(column < row, second, middle))
        for h in range(2):
            for x in range(4):
                packed[2 * x + h, t] = p[8 * h:8 * h + 8]


def analysis_kernel(
    mine, other, forecasts, modes, out,
    packed, crosses, zf, zh, fh, held, arrival,
):
    fetch = pltpu.make_async_copy(forecasts, held, arrival)
    fetch.start()
    group = lax.axis_index("members")
    core = lax.axis_index("core")
    for g in range(GROUPS):
        for t in range(PACKS):
            at = pl.multiple_of(g * MD + core * 8, 8)
            packed[t, pl.ds(at, 8), :] = mine[g, t]
            at = pl.multiple_of(g * MD + 8 - core * 8, 8)
            packed[t, pl.ds(at, 8), :] = other[g, t]
    i = lax.broadcasted_iota(jnp.int32, (M, M), 0)
    j = lax.broadcasted_iota(jnp.int32, (M, M), 1)
    diagonal = i == j
    drives = []
    square = None
    for t in range(PACKS):
        p = packed[t]
        q = p.T
        if t < L:
            drives.append(jnp.sum(jnp.where(diagonal, p, 0.0), axis=0, keepdims=True))
        for side in range(2):
            keep = (i < j) if side == 0 else (i > j)
            s = jnp.where(diagonal, 0.0, jnp.where(keep, p, q))
            s = s - jnp.where(diagonal, jnp.sum(s, axis=0, keepdims=True), 0.0)
            k = 2 * t + side
            if k >= len(PAIRS):
                crosses[k - len(PAIRS)] = s
                continue
            a, b = PAIRS[k]
            if a == b:
                s = s + jnp.where(diagonal, 1.0, 0.0)
            zf[a * M:(a + 1) * M, b * M:(b + 1) * M] = s
            if a != b:
                zf[b * M:(b + 1) * M, a * M:(a + 1) * M] = s
            part = jnp.sum(s * s, axis=0, keepdims=True) * (1.0 if a == b else 2.0)
            square = part if square is None else square + part
    norm = jnp.sqrt(jnp.sum(square, axis=1, keepdims=True))
    inverse_norm = 1.0 / norm
    own_rows = pl.ds(pl.multiple_of(group * MD, MD), MD)
    v = jnp.concatenate(
        [drives[a] - 0.5 * crosses[a, own_rows, :] for a in range(L)], axis=1
    )
    size = L * M
    z = zf[...] * inverse_norm
    for step in range(3):
        high, low = split2(z)
        zf[0:size] = z
        zh[0:size] = high
        zh[size:2 * size] = low
        vh, vl = split2(v)
        zh[2 * size:2 * size + MD] = vh
        zh[2 * size + MD:] = vl
        q = dot(zh[0:size], zh[0:size])
        fh[...] = (0.25 * q - 1.5 * zf[...]).astype(BF)
        new = dot(zh[...], fh[...])
        z = 2.25 * zf[...] + (new[0:size] + new[size:2 * size])
        v = 2.25 * v + (new[2 * size:2 * size + MD] + new[2 * size + MD:])
    high, low = split2(z)
    fh[...] = high
    zh[0:size] = low
    for step in range(2):
        vh, vl = split2(v)
        both = jnp.concatenate([vh, vl], axis=0)
        got = dot(both, fh[...])
        got = got[:MD] + (got[MD:] + dot(vh, zh[0:size]))
        v = 1.5 * v - 0.5 * got
    v = v * inverse_norm
    blocks = []
    for a in range(L):
        block = v[:, a * M:(a + 1) * M]
        blocks.append(block - jnp.mean(block, axis=1, keepdims=True))
    coeff = jnp.concatenate(blocks, axis=0)
    ch, cl = split2(coeff)
    both = jnp.concatenate([ch, cl], axis=0)
    scaled = modes[...] * (1.0 / ROOT)
    fetch.wait()
    for c in range(0, C, 2):
        block = jnp.concatenate(
            [held[:, c + k].reshape(M, LEV) for k in range(2)], axis=1
        )
        bh, bl = split2(block)
        r = dot(both, bh)
        r = r[:L * MD] + (r[L * MD:] + dot(ch, bl))
        for k in range(2):
            total = held[group, c + k]
            for a in range(L):
                total = total + scaled[a:a + 1] * r[a * MD:(a + 1) * MD, k * LEV:(k + 1) * LEV]
            out[:, c + k, :] = total


def call(kernel, outs, scratch, total, smem=0, remain=None, name=None):
    spaces = [pltpu.SMEM if n < smem else pltpu.HBM if n == remain else pltpu.VMEM for n in range(total)]
    return pl.pallas_call(
        kernel,
        out_shape=outs,
        in_specs=[pl.BlockSpec(memory_space=s) for s in spaces],
        out_specs=jax.tree.map(lambda _: pl.BlockSpec(memory_space=pltpu.VMEM), outs),
        scratch_shapes=scratch,
        compiler_params=pltpu.CompilerParams(vmem_limit_bytes=VMEM_LIMIT if remain is None else FULL_LIMIT),
        name=name,
    )


def swap(x, axes):
    return lax.all_to_all(x, axes, split_axis=0, concat_axis=0, tiled=True)


def summed_copies(x, copies):
    total = jnp.sum(x, axis=0)
    return jnp.broadcast_to(total[None], (copies,) + total.shape)


def per_device(
    ensemble, neighbours, regime, norm_gain, up_weight, down_weight, vertical_modes,
    obs_col, obs_lev, obs_val, obs_err,
):
    shape = jax.ShapeDtypeStruct
    forward = [(n, n + 1) for n in range(63)]
    backward = [(b, a) for a, b in forward]
    low = lax.ppermute(ensemble[:, C - HALO:, :], BANDS, forward)
    high = lax.ppermute(ensemble[:, :HALO, :], BANDS, backward)
    lev = obs_lev.reshape(1, OBS)
    col = obs_col.reshape(1, OBS)
    val = obs_val.reshape(1, OBS)
    err = obs_err.reshape(1, OBS)
    own, up, down, one_hot, which, at_obs, place = call(
        prepare_kernel,
        [
            shape((C, MD, LEV), F32), shape((E, LEV, FF), BF), shape((E, FF, LEV), BF),
            shape((LEV, OBS), BF), shape((C * MD, LEV), jnp.int32), shape((8, OBS), F32),
            shape((1, OBS), jnp.int32),
        ],
        [], 10, smem=1, name="prepare",
    )(
        regime, ensemble, up_weight, down_weight, col, lev, val, err, vertical_modes,
        norm_gain.reshape(1, LEV),
    )
    forecast, values = call(
        forecast_kernel,
        [shape((C, MD, LEV), F32), shape((GROUPS, MD, OBS), F32)],
        [pltpu.VMEM((C + 2 * HALO, MD, LEV), F32)],
        10, smem=1, name="forecast",
    )(neighbours, own, low, high, up, down, one_hot, which, at_obs, place)
    values = swap(values, "members")
    gathered = lax.all_gather(forecast, "members")
    packed = call(
        gram_kernel,
        shape((8, PACKS, 8, M), F32),
        [pltpu.VMEM((M, OBS), F32)],
        2, name="gram",
    )(values, at_obs)
    packed = swap(packed, ("x", "core"))
    packed = swap(summed_copies(packed, 8), "z")
    mine = swap(summed_copies(packed, GROUPS), "members")
    other = lax.ppermute(mine, "core", [(0, 1), (1, 0)])
    size = L * M
    return call(
        analysis_kernel,
        shape((MD, C, LEV), F32),
        [
            pltpu.VMEM((PACKS, M, M), F32),
            pltpu.VMEM((L, M, M), F32),
            pltpu.VMEM((size, size), F32),
            pltpu.VMEM((2 * size + 2 * MD, size), BF),
            pltpu.VMEM((size, size), BF),
            pltpu.VMEM((GROUPS, C, MD, LEV), F32),
            pltpu.SemaphoreType.DMA,
        ],
        4, remain=2, name="analysis",
    )(mine, other, gathered, vertical_modes)


def solution(mesh):
    fine = Mesh(mesh.devices.reshape(8, 8, 4, 2), ("members",) + BANDS)
    in_specs = (
        P("members", BANDS, None),
        P(BANDS, None),
        P(BANDS),
        P(),
        P(),
        P(),
        P(),
        P(BANDS),
        P(BANDS),
        P(BANDS),
        P(BANDS),
    )
    out_specs = P("members", BANDS, None)
    return jax.shard_map(
        per_device, mesh=fine, in_specs=in_specs, out_specs=out_specs, check_vma=False
    )
```

```python
import functools
import math

import jax
import jax.numpy as jnp
from jax import lax
from jax.experimental import pallas as pl
from jax.experimental.pallas import tpu as pltpu
from jax.sharding import Mesh, PartitionSpec as P

E = 4
L = 4
NB = 4
HALO = 8
M = 128
LEV = 128
FF = 512
C = 16
MD = 16
OBS = 256
GROUPS = 8
PACKS = 7
PAIRS = [(a, b) for a in range(L) for b in range(a, L)]
ROOT = math.sqrt(L * M - 1)
BF = jnp.bfloat16
F32 = jnp.float32
VMEM_LIMIT = 40 * 1024 * 1024
BANDS = ("z", "x", "core")


def dot(a, b):
    return jnp.dot(a, b, preferred_element_type=F32)


def dot_nt(a, b):
    return lax.dot_general(a, b, (((1,), (1,)), ((), ())), preferred_element_type=F32)


def split2(a):
    high = a.astype(BF)
    return high, (a - high.astype(F32)).astype(BF)


def split3(a):
    high = a.astype(BF)
    rest = a - high.astype(F32)
    middle = rest.astype(BF)
    return high, middle, (rest - middle.astype(F32)).astype(BF)


def prepare_kernel(
    regime, ens, up, down, col, lev, val, err, modes, gain,
    own_out, up_out, down_out, hot_out, regs_out, w_out, place_out,
):
    band = (lax.axis_index("z") * 4 + lax.axis_index("x")) * 2 + lax.axis_index("core")
    place_out[...] = col[...] - band * C
    for c in range(C):
        own_out[c] = ens[:, c, :]
        regs_out[c * MD:(c + 1) * MD, :] = jnp.full((MD, LEV), regime[c], jnp.int32)
    up_out[...] = up[...]
    down_out[...] = down[...]
    one_hot = (lax.broadcasted_iota(jnp.int32, (LEV, OBS), 0) == lev[...]).astype(F32).astype(BF)
    hot_out[...] = one_hot
    at_obs = None
    for part in split3(modes[...]):
        got = dot(part, one_hot)
        at_obs = got if at_obs is None else at_obs + got
    w_out[0:L, :] = at_obs
    w_out[L:L + 1, :] = val[...] / err[...]
    w_out[L + 1:L + 2, :] = err[...]
    w_out[L + 2:L + 3, 0:LEV] = gain[...]


def forecast_kernel(
    nb, own_columns, low, high, up, down, one_hot, which_ref, rows_in, place_in,
    f_out, v_out, wide,
):
    band = (lax.axis_index("z") * 4 + lax.axis_index("x")) * 2 + lax.axis_index("core")
    wide[HALO:HALO + C] = own_columns[...]
    for c in range(HALO):
        wide[c] = low[:, c, :]
        wide[HALO + C + c] = high[:, c, :]
    start = band * C - HALO
    rows = []
    for c in range(C):
        total = wide[nb[c, 0] - start]
        for k in range(1, NB):
            total = total + wide[nb[c, k] - start]
        own = own_columns[c]
        rows.append(own + 0.5 * (0.25 * total - own))
    flat = jnp.concatenate(rows, axis=0)
    inv_rms = lax.rsqrt(jnp.mean(flat * flat, axis=1, keepdims=True) + 1e-05)
    normed = (flat * inv_rms * rows_in[L + 2:L + 3, 0:LEV]).astype(BF)
    which = which_ref[...]
    which4 = jnp.concatenate([which] * (FF // LEV), axis=1)
    pre = dot(normed, up[0])
    for e in range(1, E):
        pre = jnp.where(which4 == e, dot(normed, up[e]), pre)
    hidden = pre / (1.0 + jnp.exp(-pre))
    tendency = None
    for e in range(E):
        part = dot(jnp.where(which4 == e, hidden, 0.0).astype(BF), down[e])
        tendency = part if tendency is None else tendency + part
    out = flat + tendency
    f_out[...] = out.reshape(C, MD, LEV)

    picked = None
    for part in split3(out):
        got = dot(part, one_hot[...])
        picked = got if picked is None else picked + got
    place = place_in[...]
    sampled = jnp.zeros((MD, OBS), F32)
    for c in range(C):
        sampled = sampled + jnp.where(place == c, picked[c * MD:(c + 1) * MD, :], 0.0)
    sampled = sampled / rows_in[L + 1:L + 2, :]
    for g in range(GROUPS):
        v_out[g] = sampled


def gram_kernel(values, at_obs, own_forecast, far_forecast, packed, pair, centred):
    pair[0] = own_forecast[...]
    pair[1] = far_forecast[...]
    group = lax.axis_index("members")
    raw = values[...].reshape(M, OBS)
    mean = jnp.sum(raw, axis=0, keepdims=True) * (1.0 / M)
    pert = raw - mean
    again = jnp.sum(pert, axis=0, keepdims=True) * (1.0 / M)
    pert = pert - again
    centred[...] = pert
    innovation = at_obs[L:L + 1, :] - (mean + again)
    own = centred[pl.ds(pl.multiple_of(group * MD, MD), MD), :]
    w = at_obs[...]
    weights = [w[a:a + 1] * w[b:b + 1] * (1.0 / (L * M - 1)) for a, b in PAIRS]
    weights += [w[a:a + 1] * (1.0 / ROOT) for a in range(L)]
    left = jnp.concatenate([own * f for f in weights], axis=0)
    right = jnp.concatenate(
        [pert, jnp.broadcast_to(innovation, (M, OBS))], axis=0
    )
    lh, ll = split2(left)
    rh, rl = split2(right)
    s = dot_nt(lh, rh) + (dot_nt(lh, rl) + dot_nt(ll, rh))
    row = lax.broadcasted_iota(jnp.int32, (MD, M), 0) + group * MD
    column = lax.broadcasted_iota(jnp.int32, (MD, M), 1)
    for t in range(PACKS):
        first = s[(2 * t) * MD:(2 * t + 1) * MD, :M]
        second = s[(2 * t + 1) * MD:(2 * t + 2) * MD, :M]
        if t < L:
            k = len(PAIRS) + t
            middle = s[k * MD:(k + 1) * MD, M:]
        else:
            middle = jnp.zeros((MD, M), F32)
        p = jnp.where(column > row, first, jnp.where(column < row, second, middle))
        for h in range(2):
            for x in range(4):
                packed[2 * x + h, t] = p[8 * h:8 * h + 8]


def middle_kernel(parts, pair, far_pair, copies, quad):
    total = parts[0]
    for n in range(1, parts.shape[0]):
        total = total + parts[n]
    for n in range(copies.shape[0]):
        copies[n] = total
    quad[0:2] = pair[...]
    quad[2:4] = far_pair[...]


def analysis_kernel(
    mine, other, quad, far_quad, modes, out,
    packed, crosses, zf, zh, fh, held,
):
    group = lax.axis_index("members")
    core = lax.axis_index("core")
    for n, offset in enumerate((0, 4, 2, 6)):
        held[group ^ offset] = quad[n]
        held[group ^ (offset + 1)] = far_quad[n]
    for g in range(GROUPS):
        for t in range(PACKS):
            at = pl.multiple_of(g * MD + core * 8, 8)
            packed[t, pl.ds(at, 8), :] = mine[g, t]
            at = pl.multiple_of(g * MD + 8 - core * 8, 8)
            packed[t, pl.ds(at, 8), :] = other[g, t]
    i = lax.broadcasted_iota(jnp.int32, (M, M), 0)
    j = lax.broadcasted_iota(jnp.int32, (M, M), 1)
    diagonal = i == j
    drives = []
    square = None
    for t in range(PACKS):
        p = packed[t]
        q = p.T
        if t < L:
            drives.append(jnp.sum(jnp.where(diagonal, p, 0.0), axis=0, keepdims=True))
        for side in range(2):
            keep = (i < j) if side == 0 else (i > j)
            s = jnp.where(diagonal, 0.0, jnp.where(keep, p, q))
            s = s - jnp.where(diagonal, jnp.sum(s, axis=0, keepdims=True), 0.0)
            k = 2 * t + side
            if k >= len(PAIRS):
                crosses[k - len(PAIRS)] = s
                continue
            a, b = PAIRS[k]
            if a == b:
                s = s + jnp.where(diagonal, 1.0, 0.0)
            zf[a * M:(a + 1) * M, b * M:(b + 1) * M] = s
            if a != b:
                zf[b * M:(b + 1) * M, a * M:(a + 1) * M] = s
            part = jnp.sum(s * s, axis=0, keepdims=True) * (1.0 if a == b else 2.0)
            square = part if square is None else square + part
    norm = jnp.sqrt(jnp.sum(square, axis=1, keepdims=True))
    inverse_norm = 1.0 / norm
    own_rows = pl.ds(pl.multiple_of(group * MD, MD), MD)
    v = jnp.concatenate(
        [drives[a] - 0.5 * crosses[a, own_rows, :] for a in range(L)], axis=1
    )
    size = L * M
    z = zf[...] * inverse_norm
    for step in range(3):
        high, low = split2(z)
        zf[0:size] = z
        zh[0:size] = high
        zh[size:2 * size] = low
        vh, vl = split2(v)
        zh[2 * size:2 * size + MD] = vh
        zh[2 * size + MD:] = vl
        q = dot(zh[0:size], zh[0:size])
        fh[...] = (0.25 * q - 1.5 * zf[...]).astype(BF)
        new = dot(zh[...], fh[...])
        z = 2.25 * zf[...] + (new[0:size] + new[size:2 * size])
        v = 2.25 * v + (new[2 * size:2 * size + MD] + new[2 * size + MD:])
    high, low = split2(z)
    fh[...] = high
    zh[0:size] = low
    for step in range(2):
        vh, vl = split2(v)
        both = jnp.concatenate([vh, vl], axis=0)
        got = dot(both, fh[...])
        got = got[:MD] + (got[MD:] + dot(vh, zh[0:size]))
        v = 1.5 * v - 0.5 * got
    v = v * inverse_norm
    blocks = []
    for a in range(L):
        block = v[:, a * M:(a + 1) * M]
        blocks.append(block - jnp.mean(block, axis=1, keepdims=True))
    coeff = jnp.concatenate(blocks, axis=0)
    ch, cl = split2(coeff)
    both = jnp.concatenate([ch, cl], axis=0)
    scaled = modes[...] * (1.0 / ROOT)
    for c in range(0, C, 2):
        block = jnp.concatenate(
            [held[:, c + k].reshape(M, LEV) for k in range(2)], axis=1
        )
        bh, bl = split2(block)
        r = dot(both, bh)
        r = r[:L * MD] + (r[L * MD:] + dot(ch, bl))
        for k in range(2):
            total = held[group, c + k]
            for a in range(L):
                total = total + scaled[a:a + 1] * r[a * MD:(a + 1) * MD, k * LEV:(k + 1) * LEV]
            out[:, c + k, :] = total


def call(kernel, outs, scratch, total, smem=0, name=None):
    spaces = [pltpu.SMEM if n < smem else pltpu.VMEM for n in range(total)]
    return pl.pallas_call(
        kernel,
        out_shape=outs,
        in_specs=[pl.BlockSpec(memory_space=s) for s in spaces],
        out_specs=jax.tree.map(lambda _: pl.BlockSpec(memory_space=pltpu.VMEM), outs),
        scratch_shapes=scratch,
        compiler_params=pltpu.CompilerParams(vmem_limit_bytes=VMEM_LIMIT),
        name=name,
    )


def swap(x, axes):
    return lax.all_to_all(x, axes, split_axis=0, concat_axis=0, tiled=True)


def partner(x, distance):
    return lax.ppermute(x, "members", [(n, n ^ distance) for n in range(GROUPS)])


def summed_copies(x, copies):
    total = jnp.sum(x, axis=0)
    return jnp.broadcast_to(total[None], (copies,) + total.shape)


def per_device(
    ensemble, neighbours, regime, norm_gain, up_weight, down_weight, vertical_modes,
    obs_col, obs_lev, obs_val, obs_err,
):
    shape = jax.ShapeDtypeStruct
    forward = [(n, n + 1) for n in range(63)]
    backward = [(b, a) for a, b in forward]
    low = lax.ppermute(ensemble[:, C - HALO:, :], BANDS, forward)
    high = lax.ppermute(ensemble[:, :HALO, :], BANDS, backward)
    lev = obs_lev.reshape(1, OBS)
    col = obs_col.reshape(1, OBS)
    val = obs_val.reshape(1, OBS)
    err = obs_err.reshape(1, OBS)
    own, up, down, one_hot, which, at_obs, place = call(
        prepare_kernel,
        [
            shape((C, MD, LEV), F32), shape((E, LEV, FF), BF), shape((E, FF, LEV), BF),
            shape((LEV, OBS), BF), shape((C * MD, LEV), jnp.int32), shape((8, OBS), F32),
            shape((1, OBS), jnp.int32),
        ],
        [], 10, smem=1, name="prepare",
    )(
        regime, ensemble, up_weight, down_weight, col, lev, val, err, vertical_modes,
        norm_gain.reshape(1, LEV),
    )
    forecast, values = call(
        forecast_kernel,
        [shape((C, MD, LEV), F32), shape((GROUPS, MD, OBS), F32)],
        [pltpu.VMEM((C + 2 * HALO, MD, LEV), F32)],
        10, smem=1, name="forecast",
    )(neighbours, own, low, high, up, down, one_hot, which, at_obs, place)
    far = partner(forecast, 4)
    values = swap(values, "members")
    packed, pair = call(
        gram_kernel,
        [shape((8, PACKS, 8, M), F32), shape((2, C, MD, LEV), F32)],
        [pltpu.VMEM((M, OBS), F32)],
        4, name="gram",
    )(values, at_obs, forecast, far)
    far_pair = partner(pair, 2)
    packed = swap(packed, ("x", "core"))
    packed, quad = call(
        middle_kernel,
        [shape((8, PACKS, 8, M), F32), shape((4, C, MD, LEV), F32)],
        [], 3, name="middle",
    )(packed, pair, far_pair)
    far_quad = partner(quad, 1)
    packed = swap(packed, "z")
    packed, far_quad = lax.optimization_barrier((packed, far_quad))
    mine = swap(summed_copies(packed, GROUPS), "members")
    other = lax.ppermute(mine, "core", [(0, 1), (1, 0)])
    size = L * M
    return call(
        analysis_kernel,
        shape((MD, C, LEV), F32),
        [
            pltpu.VMEM((PACKS, M, M), F32),
            pltpu.VMEM((L, M, M), F32),
            pltpu.VMEM((size, size), F32),
            pltpu.VMEM((2 * size + 2 * MD, size), BF),
            pltpu.VMEM((size, size), BF),
            pltpu.VMEM((GROUPS, C, MD, LEV), F32),
        ],
        5, name="analysis",
    )(mine, other, quad, far_quad, vertical_modes)


def solution(mesh):
    fine = Mesh(mesh.devices.reshape(8, 8, 4, 2), ("members",) + BANDS)
    in_specs = (
        P("members", BANDS, None),
        P(BANDS, None),
        P(BANDS),
        P(),
        P(),
        P(),
        P(),
        P(BANDS),
        P(BANDS),
        P(BANDS),
        P(BANDS),
    )
    out_specs = P("members", BANDS, None)
    return jax.shard_map(
        per_device, mesh=fine, in_specs=in_specs, out_specs=out_specs, check_vma=False
    )
```

```python
import functools
import math

import jax
import jax.numpy as jnp
from jax import lax
from jax.experimental import pallas as pl
from jax.experimental.pallas import tpu as pltpu
from jax.sharding import Mesh, PartitionSpec as P

E = 4
L = 4
NB = 4
HALO = 8
M = 128
LEV = 128
FF = 512
C = 16
MD = 16
OBS = 256
GROUPS = 8
PACKS = 7
PAIRS = [(a, b) for a in range(L) for b in range(a, L)]
ROOT = math.sqrt(L * M - 1)
BF = jnp.bfloat16
F32 = jnp.float32
VMEM_LIMIT = 40 * 1024 * 1024
BANDS = ("z", "x", "core")


def dot(a, b):
    return jnp.dot(a, b, preferred_element_type=F32)


def dot_nt(a, b):
    return lax.dot_general(a, b, (((1,), (1,)), ((), ())), preferred_element_type=F32)


def split2(a):
    high = a.astype(BF)
    return high, (a - high.astype(F32)).astype(BF)


def split3(a):
    high = a.astype(BF)
    rest = a - high.astype(F32)
    middle = rest.astype(BF)
    return high, middle, (rest - middle.astype(F32)).astype(BF)


def prepare_kernel(
    regime, ens, up, down, col, lev, val, err, modes, gain,
    own_out, up_out, down_out, hot_out, regs_out, w_out, place_out,
):
    band = (lax.axis_index("z") * 4 + lax.axis_index("x")) * 2 + lax.axis_index("core")
    place_out[...] = col[...] - band * C
    for c in range(C):
        own_out[c] = ens[:, c, :]
        regs_out[c * MD:(c + 1) * MD, :] = jnp.full((MD, LEV), regime[c], jnp.int32)
    up_out[...] = up[...]
    down_out[...] = down[...]
    one_hot = (lax.broadcasted_iota(jnp.int32, (LEV, OBS), 0) == lev[...]).astype(F32).astype(BF)
    hot_out[...] = one_hot
    at_obs = None
    for part in split3(modes[...]):
        got = dot(part, one_hot)
        at_obs = got if at_obs is None else at_obs + got
    w_out[0:L, :] = at_obs
    w_out[L:L + 1, :] = val[...] / err[...]
    w_out[L + 1:L + 2, :] = err[...]
    w_out[L + 2:L + 3, 0:LEV] = gain[...]


def forecast_kernel(
    nb, own_columns, low, high, up, down, one_hot, which_ref, rows_in, place_in,
    f_out, v_out, wide,
):
    band = (lax.axis_index("z") * 4 + lax.axis_index("x")) * 2 + lax.axis_index("core")
    wide[HALO:HALO + C] = own_columns[...]
    for c in range(HALO):
        wide[c] = low[:, c, :]
        wide[HALO + C + c] = high[:, c, :]
    start = band * C - HALO
    rows = []
    for c in range(C):
        total = wide[nb[c, 0] - start]
        for k in range(1, NB):
            total = total + wide[nb[c, k] - start]
        own = own_columns[c]
        rows.append(own + 0.5 * (0.25 * total - own))
    flat = jnp.concatenate(rows, axis=0)
    inv_rms = lax.rsqrt(jnp.mean(flat * flat, axis=1, keepdims=True) + 1e-05)
    normed = (flat * inv_rms * rows_in[L + 2:L + 3, 0:LEV]).astype(BF)
    which = which_ref[...]
    which4 = jnp.concatenate([which] * (FF // LEV), axis=1)
    pre = dot(normed, up[0])
    for e in range(1, E):
        pre = jnp.where(which4 == e, dot(normed, up[e]), pre)
    hidden = pre / (1.0 + jnp.exp(-pre))
    tendency = None
    for e in range(E):
        part = dot(jnp.where(which4 == e, hidden, 0.0).astype(BF), down[e])
        tendency = part if tendency is None else tendency + part
    out = flat + tendency
    f_out[...] = out.reshape(C, MD, LEV)

    picked = None
    for part in split3(out):
        got = dot(part, one_hot[...])
        picked = got if picked is None else picked + got
    place = place_in[...]
    sampled = jnp.zeros((MD, OBS), F32)
    for c in range(C):
        sampled = sampled + jnp.where(place == c, picked[c * MD:(c + 1) * MD, :], 0.0)
    sampled = sampled / rows_in[L + 1:L + 2, :]
    for g in range(GROUPS):
        v_out[g] = sampled


def gram_kernel(values, at_obs, packed, centred):
    group = lax.axis_index("members")
    raw = values[...].reshape(M, OBS)
    mean = jnp.sum(raw, axis=0, keepdims=True) * (1.0 / M)
    pert = raw - mean
    again = jnp.sum(pert, axis=0, keepdims=True) * (1.0 / M)
    pert = pert - again
    centred[...] = pert
    innovation = at_obs[L:L + 1, :] - (mean + again)
    own = centred[pl.ds(pl.multiple_of(group * MD, MD), MD), :]
    w = at_obs[...]
    weights = [w[a:a + 1] * w[b:b + 1] * (1.0 / (L * M - 1)) for a, b in PAIRS]
    weights += [w[a:a + 1] * (1.0 / ROOT) for a in range(L)]
    left = jnp.concatenate([own * f for f in weights], axis=0)
    right = jnp.concatenate(
        [pert, jnp.broadcast_to(innovation, (M, OBS))], axis=0
    )
    lh, ll = split2(left)
    rh, rl = split2(right)
    s = dot_nt(lh, rh) + (dot_nt(lh, rl) + dot_nt(ll, rh))
    row = lax.broadcasted_iota(jnp.int32, (MD, M), 0) + group * MD
    column = lax.broadcasted_iota(jnp.int32, (MD, M), 1)
    for t in range(PACKS):
        first = s[(2 * t) * MD:(2 * t + 1) * MD, :M]
        second = s[(2 * t + 1) * MD:(2 * t + 2) * MD, :M]
        if t < L:
            k = len(PAIRS) + t
            middle = s[k * MD:(k + 1) * MD, M:]
        else:
            middle = jnp.zeros((MD, M), F32)
        p = jnp.where(column > row, first, jnp.where(column < row, second, middle))
        for h in range(2):
            for x in range(4):
                packed[2 * x + h, t] = p[8 * h:8 * h + 8]


def middle_kernel(parts, own, far2, far4, far6, copies, quad):
    total = parts[0]
    for n in range(1, parts.shape[0]):
        total = total + parts[n]
    for n in range(copies.shape[0]):
        copies[n] = total
    for n, block in enumerate((own, far2, far4, far6)):
        quad[n] = block[...]


def analysis_kernel(
    mine, other, quad, far_quad, modes, out,
    packed, crosses, zf, zh, fh, held,
):
    group = lax.axis_index("members")
    core = lax.axis_index("core")
    for n, offset in enumerate((0, 2, 4, 6)):
        held[group ^ offset] = quad[n]
        held[group ^ (offset + 1)] = far_quad[n]
    for g in range(GROUPS):
        for t in range(PACKS):
            at = pl.multiple_of(g * MD + core * 8, 8)
            packed[t, pl.ds(at, 8), :] = mine[g, t]
            at = pl.multiple_of(g * MD + 8 - core * 8, 8)
            packed[t, pl.ds(at, 8), :] = other[g, t]
    i = lax.broadcasted_iota(jnp.int32, (M, M), 0)
    j = lax.broadcasted_iota(jnp.int32, (M, M), 1)
    diagonal = i == j
    drives = []
    square = None
    for t in range(PACKS):
        p = packed[t]
        q = p.T
        if t < L:
            drives.append(jnp.sum(jnp.where(diagonal, p, 0.0), axis=0, keepdims=True))
        for side in range(2):
            keep = (i < j) if side == 0 else (i > j)
            s = jnp.where(diagonal, 0.0, jnp.where(keep, p, q))
            s = s - jnp.where(diagonal, jnp.sum(s, axis=0, keepdims=True), 0.0)
            k = 2 * t + side
            if k >= len(PAIRS):
                crosses[k - len(PAIRS)] = s
                continue
            a, b = PAIRS[k]
            if a == b:
                s = s + jnp.where(diagonal, 1.0, 0.0)
            zf[a * M:(a + 1) * M, b * M:(b + 1) * M] = s
            if a != b:
                zf[b * M:(b + 1) * M, a * M:(a + 1) * M] = s
            part = jnp.sum(s * s, axis=0, keepdims=True) * (1.0 if a == b else 2.0)
            square = part if square is None else square + part
    norm = jnp.sqrt(jnp.sum(square, axis=1, keepdims=True))
    inverse_norm = 1.0 / norm
    own_rows = pl.ds(pl.multiple_of(group * MD, MD), MD)
    v = jnp.concatenate(
        [drives[a] - 0.5 * crosses[a, own_rows, :] for a in range(L)], axis=1
    )
    size = L * M
    z = zf[...] * inverse_norm
    for step in range(3):
        high, low = split2(z)
        zf[0:size] = z
        zh[0:size] = high
        zh[size:2 * size] = low
        vh, vl = split2(v)
        zh[2 * size:2 * size + MD] = vh
        zh[2 * size + MD:] = vl
        q = dot(zh[0:size], zh[0:size])
        fh[...] = (0.25 * q - 1.5 * zf[...]).astype(BF)
        new = dot(zh[...], fh[...])
        z = 2.25 * zf[...] + (new[0:size] + new[size:2 * size])
        v = 2.25 * v + (new[2 * size:2 * size + MD] + new[2 * size + MD:])
    high, low = split2(z)
    fh[...] = high
    zh[0:size] = low
    for step in range(2):
        vh, vl = split2(v)
        both = jnp.concatenate([vh, vl], axis=0)
        got = dot(both, fh[...])
        got = got[:MD] + (got[MD:] + dot(vh, zh[0:size]))
        v = 1.5 * v - 0.5 * got
    v = v * inverse_norm
    blocks = []
    for a in range(L):
        block = v[:, a * M:(a + 1) * M]
        blocks.append(block - jnp.mean(block, axis=1, keepdims=True))
    coeff = jnp.concatenate(blocks, axis=0)
    ch, cl = split2(coeff)
    both = jnp.concatenate([ch, cl], axis=0)
    scaled = modes[...] * (1.0 / ROOT)
    for c in range(0, C, 2):
        block = jnp.concatenate(
            [held[:, c + k].reshape(M, LEV) for k in range(2)], axis=1
        )
        bh, bl = split2(block)
        r = dot(both, bh)
        r = r[:L * MD] + (r[L * MD:] + dot(ch, bl))
        for k in range(2):
            total = held[group, c + k]
            for a in range(L):
                total = total + scaled[a:a + 1] * r[a * MD:(a + 1) * MD, k * LEV:(k + 1) * LEV]
            out[:, c + k, :] = total


def call(kernel, outs, scratch, total, smem=0, name=None):
    spaces = [pltpu.SMEM if n < smem else pltpu.VMEM for n in range(total)]
    return pl.pallas_call(
        kernel,
        out_shape=outs,
        in_specs=[pl.BlockSpec(memory_space=s) for s in spaces],
        out_specs=jax.tree.map(lambda _: pl.BlockSpec(memory_space=pltpu.VMEM), outs),
        scratch_shapes=scratch,
        compiler_params=pltpu.CompilerParams(vmem_limit_bytes=VMEM_LIMIT),
        name=name,
    )


def swap(x, axes):
    return lax.all_to_all(x, axes, split_axis=0, concat_axis=0, tiled=True)


def partner(x, distance):
    return lax.ppermute(x, "members", [(n, n ^ distance) for n in range(GROUPS)])


def summed_copies(x, copies):
    total = jnp.sum(x, axis=0)
    return jnp.broadcast_to(total[None], (copies,) + total.shape)


def per_device(
    ensemble, neighbours, regime, norm_gain, up_weight, down_weight, vertical_modes,
    obs_col, obs_lev, obs_val, obs_err,
):
    shape = jax.ShapeDtypeStruct
    forward = [(n, n + 1) for n in range(63)]
    backward = [(b, a) for a, b in forward]
    low = lax.ppermute(ensemble[:, C - HALO:, :], BANDS, forward)
    high = lax.ppermute(ensemble[:, :HALO, :], BANDS, backward)
    lev = obs_lev.reshape(1, OBS)
    col = obs_col.reshape(1, OBS)
    val = obs_val.reshape(1, OBS)
    err = obs_err.reshape(1, OBS)
    own, up, down, one_hot, which, at_obs, place = call(
        prepare_kernel,
        [
            shape((C, MD, LEV), F32), shape((E, LEV, FF), BF), shape((E, FF, LEV), BF),
            shape((LEV, OBS), BF), shape((C * MD, LEV), jnp.int32), shape((8, OBS), F32),
            shape((1, OBS), jnp.int32),
        ],
        [], 10, smem=1, name="prepare",
    )(
        regime, ensemble, up_weight, down_weight, col, lev, val, err, vertical_modes,
        norm_gain.reshape(1, LEV),
    )
    forecast, values = call(
        forecast_kernel,
        [shape((C, MD, LEV), F32), shape((GROUPS, MD, OBS), F32)],
        [pltpu.VMEM((C + 2 * HALO, MD, LEV), F32)],
        10, smem=1, name="forecast",
    )(neighbours, own, low, high, up, down, one_hot, which, at_obs, place)
    values = swap(values, "members")
    packed = call(
        gram_kernel,
        shape((8, PACKS, 8, M), F32),
        [pltpu.VMEM((M, OBS), F32)],
        2, name="gram",
    )(values, at_obs)
    packed, forecast = lax.optimization_barrier((packed, forecast))
    far = [partner(forecast, distance) for distance in (2, 4, 6)]
    packed = swap(packed, ("x", "core"))
    packed, quad = call(
        middle_kernel,
        [shape((8, PACKS, 8, M), F32), shape((4, C, MD, LEV), F32)],
        [], 5, name="middle",
    )(packed, forecast, *far)
    far_quad = partner(quad, 1)
    packed = swap(packed, "z")
    packed, far_quad = lax.optimization_barrier((packed, far_quad))
    mine = swap(summed_copies(packed, GROUPS), "members")
    other = lax.ppermute(mine, "core", [(0, 1), (1, 0)])
    size = L * M
    return call(
        analysis_kernel,
        shape((MD, C, LEV), F32),
        [
            pltpu.VMEM((PACKS, M, M), F32),
            pltpu.VMEM((L, M, M), F32),
            pltpu.VMEM((size, size), F32),
            pltpu.VMEM((2 * size + 2 * MD, size), BF),
            pltpu.VMEM((size, size), BF),
            pltpu.VMEM((GROUPS, C, MD, LEV), F32),
        ],
        5, name="analysis",
    )(mine, other, quad, far_quad, vertical_modes)


def solution(mesh):
    fine = Mesh(mesh.devices.reshape(8, 8, 4, 2), ("members",) + BANDS)
    in_specs = (
        P("members", BANDS, None),
        P(BANDS, None),
        P(BANDS),
        P(),
        P(),
        P(),
        P(),
        P(BANDS),
        P(BANDS),
        P(BANDS),
        P(BANDS),
    )
    out_specs = P("members", BANDS, None)
    return jax.shard_map(
        per_device, mesh=fine, in_specs=in_specs, out_specs=out_specs, check_vma=False
    )
```

```python
import functools
import math

import jax
import jax.numpy as jnp
from jax import lax
from jax.experimental import pallas as pl
from jax.experimental.pallas import tpu as pltpu
from jax.sharding import Mesh, PartitionSpec as P

E = 4
L = 4
NB = 4
HALO = 8
M = 128
LEV = 128
FF = 512
C = 16
MD = 16
OBS = 256
GROUPS = 8
PACKS = 7
PAIRS = [(a, b) for a in range(L) for b in range(a, L)]
ROOT = math.sqrt(L * M - 1)
BF = jnp.bfloat16
F32 = jnp.float32
VMEM_LIMIT = 40 * 1024 * 1024
BANDS = ("z", "x", "core")


def dot(a, b):
    return jnp.dot(a, b, preferred_element_type=F32)


def dot_nt(a, b):
    return lax.dot_general(a, b, (((1,), (1,)), ((), ())), preferred_element_type=F32)


def split2(a):
    high = a.astype(BF)
    return high, (a - high.astype(F32)).astype(BF)


def split3(a):
    high = a.astype(BF)
    rest = a - high.astype(F32)
    middle = rest.astype(BF)
    return high, middle, (rest - middle.astype(F32)).astype(BF)


def prepare_kernel(
    regime, ens, up, down, col, lev, val, err, modes, gain,
    own_out, up_out, down_out, hot_out, regs_out, w_out, place_out,
):
    band = (lax.axis_index("z") * 4 + lax.axis_index("x")) * 2 + lax.axis_index("core")
    place_out[...] = col[...] - band * C
    for c in range(C):
        own_out[c] = ens[:, c, :]
        regs_out[c * MD:(c + 1) * MD, :] = jnp.full((MD, LEV), regime[c], jnp.int32)
    up_out[...] = up[...]
    down_out[...] = down[...]
    one_hot = (lax.broadcasted_iota(jnp.int32, (LEV, OBS), 0) == lev[...]).astype(F32).astype(BF)
    hot_out[...] = one_hot
    at_obs = None
    for part in split3(modes[...]):
        got = dot(part, one_hot)
        at_obs = got if at_obs is None else at_obs + got
    w_out[0:L, :] = at_obs
    w_out[L:L + 1, :] = val[...] / err[...]
    w_out[L + 1:L + 2, :] = err[...]
    w_out[L + 2:L + 3, 0:LEV] = gain[...]


def forecast_kernel(
    nb, own_columns, low, high, up, down, one_hot, which_ref, rows_in, place_in,
    v_out, wide,
):
    band = (lax.axis_index("z") * 4 + lax.axis_index("x")) * 2 + lax.axis_index("core")
    wide[HALO:HALO + C] = own_columns[...]
    for c in range(HALO):
        wide[c] = low[:, c, :]
        wide[HALO + C + c] = high[:, c, :]
    start = band * C - HALO
    rows = []
    for c in range(C):
        total = wide[nb[c, 0] - start]
        for k in range(1, NB):
            total = total + wide[nb[c, k] - start]
        own = own_columns[c]
        rows.append(own + 0.5 * (0.25 * total - own))
    flat = jnp.concatenate(rows, axis=0)
    inv_rms = lax.rsqrt(jnp.mean(flat * flat, axis=1, keepdims=True) + 1e-05)
    normed = (flat * inv_rms * rows_in[L + 2:L + 3, 0:LEV]).astype(BF)
    which = which_ref[...]
    which4 = jnp.concatenate([which] * (FF // LEV), axis=1)
    pre = dot(normed, up[0])
    for e in range(1, E):
        pre = jnp.where(which4 == e, dot(normed, up[e]), pre)
    hidden = pre / (1.0 + jnp.exp(-pre))
    tendency = None
    for e in range(E):
        part = dot(jnp.where(which4 == e, hidden, 0.0).astype(BF), down[e])
        tendency = part if tendency is None else tendency + part
    out = flat + tendency
    picked = None
    for part in split3(out):
        got = dot(part, one_hot[...])
        picked = got if picked is None else picked + got
    place = place_in[...]
    sampled = jnp.zeros((MD, OBS), F32)
    for c in range(C):
        sampled = sampled + jnp.where(place == c, picked[c * MD:(c + 1) * MD, :], 0.0)
    sampled = sampled / rows_in[L + 1:L + 2, :]
    for g in range(GROUPS):
        for k in range(2):
            v_out[g, k] = sampled[:, k * LEV:(k + 1) * LEV]
            v_out[g, 2 + k] = out[(2 * g + k) * MD:(2 * g + k + 1) * MD]


def gram_kernel(values, at_obs, packed, centred):
    group = lax.axis_index("members")
    raw = jnp.concatenate([values[:, k].reshape(M, LEV) for k in range(2)], axis=1)
    mean = jnp.sum(raw, axis=0, keepdims=True) * (1.0 / M)
    pert = raw - mean
    again = jnp.sum(pert, axis=0, keepdims=True) * (1.0 / M)
    pert = pert - again
    centred[...] = pert
    innovation = at_obs[L:L + 1, :] - (mean + again)
    own = centred[pl.ds(pl.multiple_of(group * MD, MD), MD), :]
    w = at_obs[...]
    weights = [w[a:a + 1] * w[b:b + 1] * (1.0 / (L * M - 1)) for a, b in PAIRS]
    weights += [w[a:a + 1] * (1.0 / ROOT) for a in range(L)]
    left = jnp.concatenate([own * f for f in weights], axis=0)
    right = jnp.concatenate(
        [pert, jnp.broadcast_to(innovation, (M, OBS))], axis=0
    )
    lh, ll = split2(left)
    rh, rl = split2(right)
    s = dot_nt(lh, rh) + (dot_nt(lh, rl) + dot_nt(ll, rh))
    row = lax.broadcasted_iota(jnp.int32, (MD, M), 0) + group * MD
    column = lax.broadcasted_iota(jnp.int32, (MD, M), 1)
    for t in range(PACKS):
        first = s[(2 * t) * MD:(2 * t + 1) * MD, :M]
        second = s[(2 * t + 1) * MD:(2 * t + 2) * MD, :M]
        if t < L:
            k = len(PAIRS) + t
            middle = s[k * MD:(k + 1) * MD, M:]
        else:
            middle = jnp.zeros((MD, M), F32)
        p = jnp.where(column > row, first, jnp.where(column < row, second, middle))
        for h in range(2):
            for x in range(4):
                packed[2 * x + h, t] = p[8 * h:8 * h + 8]


def analysis_kernel(
    mine, other, values, modes, out,
    packed, crosses, zf, zh, fh,
):
    core = lax.axis_index("core")
    for g in range(GROUPS):
        for t in range(PACKS):
            at = pl.multiple_of(g * MD + core * 8, 8)
            packed[t, pl.ds(at, 8), :] = mine[g, t]
            at = pl.multiple_of(g * MD + 8 - core * 8, 8)
            packed[t, pl.ds(at, 8), :] = other[g, t]
    i = lax.broadcasted_iota(jnp.int32, (M, M), 0)
    j = lax.broadcasted_iota(jnp.int32, (M, M), 1)
    diagonal = i == j
    drives = []
    square = None
    for t in range(PACKS):
        p = packed[t]
        q = p.T
        if t < L:
            drives.append(jnp.sum(jnp.where(diagonal, p, 0.0), axis=0, keepdims=True))
        for side in range(2):
            keep = (i < j) if side == 0 else (i > j)
            s = jnp.where(diagonal, 0.0, jnp.where(keep, p, q))
            s = s - jnp.where(diagonal, jnp.sum(s, axis=0, keepdims=True), 0.0)
            k = 2 * t + side
            if k >= len(PAIRS):
                crosses[k - len(PAIRS)] = s
                continue
            a, b = PAIRS[k]
            if a == b:
                s = s + jnp.where(diagonal, 1.0, 0.0)
            zf[a * M:(a + 1) * M, b * M:(b + 1) * M] = s
            if a != b:
                zf[b * M:(b + 1) * M, a * M:(a + 1) * M] = s
            part = jnp.sum(s * s, axis=0, keepdims=True) * (1.0 if a == b else 2.0)
            square = part if square is None else square + part
    norm = jnp.sqrt(jnp.sum(square, axis=1, keepdims=True))
    inverse_norm = 1.0 / norm
    v = jnp.concatenate([drives[a] - 0.5 * crosses[a] for a in range(L)], axis=1)
    size = L * M
    z = zf[...] * inverse_norm
    for step in range(3):
        high, low = split2(z)
        zf[0:size] = z
        zh[0:size] = high
        zh[size:2 * size] = low
        vh, vl = split2(v)
        zh[2 * size:2 * size + M] = vh
        zh[2 * size + M:] = vl
        q = dot(zh[0:size], zh[0:size])
        fh[...] = (0.25 * q - 1.5 * zf[...]).astype(BF)
        new = dot(zh[...], fh[...])
        z = 2.25 * zf[...] + (new[0:size] + new[size:2 * size])
        v = 2.25 * v + (new[2 * size:2 * size + M] + new[2 * size + M:])
    high, low = split2(z)
    fh[...] = high
    zh[0:size] = low
    for step in range(2):
        vh, vl = split2(v)
        both = jnp.concatenate([vh, vl], axis=0)
        got = dot(both, fh[...])
        got = got[:M] + (got[M:] + dot(vh, zh[0:size]))
        v = 1.5 * v - 0.5 * got
    v = v * inverse_norm
    blocks = []
    for a in range(L):
        block = v[:, a * M:(a + 1) * M]
        blocks.append(block - jnp.mean(block, axis=1, keepdims=True))
    coeff = jnp.concatenate(blocks, axis=0)
    ch, cl = split2(coeff)
    scaled = modes[...] * (1.0 / ROOT)
    columns = [values[:, 2 + k].reshape(M, LEV) for k in range(2)]
    bh, bl = split2(jnp.concatenate(columns, axis=1))
    r = dot(ch, bh) + (dot(cl, bh) + dot(ch, bl))
    for k in range(2):
        total = columns[k]
        for a in range(L):
            total = total + scaled[a:a + 1] * r[a * M:(a + 1) * M, k * LEV:(k + 1) * LEV]
        out[:, k] = total.reshape(GROUPS, MD, LEV)


def call(kernel, outs, scratch, total, smem=0, name=None):
    spaces = [pltpu.SMEM if n < smem else pltpu.VMEM for n in range(total)]
    return pl.pallas_call(
        kernel,
        out_shape=outs,
        in_specs=[pl.BlockSpec(memory_space=s) for s in spaces],
        out_specs=jax.tree.map(lambda _: pl.BlockSpec(memory_space=pltpu.VMEM), outs),
        scratch_shapes=scratch,
        compiler_params=pltpu.CompilerParams(vmem_limit_bytes=VMEM_LIMIT),
        name=name,
    )


def swap(x, axes):
    return lax.all_to_all(x, axes, split_axis=0, concat_axis=0, tiled=True)


def summed_copies(x, copies):
    total = jnp.sum(x, axis=0)
    return jnp.broadcast_to(total[None], (copies,) + total.shape)


def per_device(
    ensemble, neighbours, regime, norm_gain, up_weight, down_weight, vertical_modes,
    obs_col, obs_lev, obs_val, obs_err,
):
    shape = jax.ShapeDtypeStruct
    forward = [(n, n + 1) for n in range(63)]
    backward = [(b, a) for a, b in forward]
    low = lax.ppermute(ensemble[:, C - HALO:, :], BANDS, forward)
    high = lax.ppermute(ensemble[:, :HALO, :], BANDS, backward)
    lev = obs_lev.reshape(1, OBS)
    col = obs_col.reshape(1, OBS)
    val = obs_val.reshape(1, OBS)
    err = obs_err.reshape(1, OBS)
    own, up, down, one_hot, which, at_obs, place = call(
        prepare_kernel,
        [
            shape((C, MD, LEV), F32), shape((E, LEV, FF), BF), shape((E, FF, LEV), BF),
            shape((LEV, OBS), BF), shape((C * MD, LEV), jnp.int32), shape((8, OBS), F32),
            shape((1, OBS), jnp.int32),
        ],
        [], 10, smem=1, name="prepare",
    )(
        regime, ensemble, up_weight, down_weight, col, lev, val, err, vertical_modes,
        norm_gain.reshape(1, LEV),
    )
    values = call(
        forecast_kernel,
        shape((GROUPS, 4, MD, LEV), F32),
        [pltpu.VMEM((C + 2 * HALO, MD, LEV), F32)],
        10, smem=1, name="forecast",
    )(neighbours, own, low, high, up, down, one_hot, which, at_obs, place)
    values = swap(values, "members")
    packed = call(
        gram_kernel,
        shape((8, PACKS, 8, M), F32),
        [pltpu.VMEM((M, OBS), F32)],
        2, name="gram",
    )(values, at_obs)
    packed = swap(packed, ("x", "core"))
    packed = swap(summed_copies(packed, 8), "z")
    mine = swap(summed_copies(packed, GROUPS), "members")
    other = lax.ppermute(mine, "core", [(0, 1), (1, 0)])
    size = L * M
    analysis = call(
        analysis_kernel,
        shape((GROUPS, 2, MD, LEV), F32),
        [
            pltpu.VMEM((PACKS, M, M), F32),
            pltpu.VMEM((L, M, M), F32),
            pltpu.VMEM((size, size), F32),
            pltpu.VMEM((2 * size + 2 * M, size), BF),
            pltpu.VMEM((size, size), BF),
        ],
        4, name="analysis",
    )(mine, other, values, vertical_modes)
    analysis = swap(analysis, "members")
    return analysis.transpose(2, 0, 1, 3).reshape(MD, C, LEV)


def solution(mesh):
    fine = Mesh(mesh.devices.reshape(8, 8, 4, 2), ("members",) + BANDS)
    in_specs = (
        P("members", BANDS, None),
        P(BANDS, None),
        P(BANDS),
        P(),
        P(),
        P(),
        P(),
        P(BANDS),
        P(BANDS),
        P(BANDS),
        P(BANDS),
    )
    out_specs = P("members", BANDS, None)
    return jax.shard_map(
        per_device, mesh=fine, in_specs=in_specs, out_specs=out_specs, check_vma=False
    )
```

```python
import functools
import math

import jax
import jax.numpy as jnp
from jax import lax
from jax.experimental import pallas as pl
from jax.experimental.pallas import tpu as pltpu
from jax.sharding import Mesh, PartitionSpec as P

E = 4
L = 4
NB = 4
HALO = 8
M = 128
LEV = 128
FF = 512
C = 16
MD = 16
OBS = 256
GROUPS = 8
PACKS = 7
PAIRS = [(a, b) for a in range(L) for b in range(a, L)]
ROOT = math.sqrt(L * M - 1)
BF = jnp.bfloat16
F32 = jnp.float32
VMEM_LIMIT = 40 * 1024 * 1024
BANDS = ("z", "x", "core")


def dot(a, b):
    return jnp.dot(a, b, preferred_element_type=F32)


def dot_nt(a, b):
    return lax.dot_general(a, b, (((1,), (1,)), ((), ())), preferred_element_type=F32)


def split2(a):
    high = a.astype(BF)
    return high, (a - high.astype(F32)).astype(BF)


def split3(a):
    high = a.astype(BF)
    rest = a - high.astype(F32)
    middle = rest.astype(BF)
    return high, middle, (rest - middle.astype(F32)).astype(BF)


def prepare_kernel(
    regime, ens, up, down, col, lev, val, err, modes, gain,
    own_out, up_out, down_out, hot_out, regs_out, w_out, place_out,
):
    band = (lax.axis_index("z") * 4 + lax.axis_index("x")) * 2 + lax.axis_index("core")
    place_out[...] = col[...] - band * C
    for c in range(C):
        own_out[c] = ens[:, c, :]
        regs_out[c * MD:(c + 1) * MD, :] = jnp.full((MD, LEV), regime[c], jnp.int32)
    up_out[...] = up[...]
    down_out[...] = down[...]
    one_hot = (lax.broadcasted_iota(jnp.int32, (LEV, OBS), 0) == lev[...]).astype(F32).astype(BF)
    hot_out[...] = one_hot
    at_obs = None
    for part in split3(modes[...]):
        got = dot(part, one_hot)
        at_obs = got if at_obs is None else at_obs + got
    w_out[0:L, :] = at_obs
    w_out[L:L + 1, :] = val[...] / err[...]
    w_out[L + 1:L + 2, :] = err[...]
    w_out[L + 2:L + 3, 0:LEV] = gain[...]


def forecast_kernel(
    nb, own_columns, inner, outer, up, down, one_hot, which_ref, rows_in, place_in,
    v_out, wide,
):
    core = lax.axis_index("core")
    band = (lax.axis_index("z") * 4 + lax.axis_index("x")) * 2 + core
    wide[HALO:HALO + C] = own_columns[...]
    inner_at = (1 - core) * (HALO + C)
    outer_at = core * (HALO + C)
    for c in range(HALO):
        wide[inner_at + c] = inner[:, c, :]
        wide[outer_at + c] = outer[:, c, :]
    start = band * C - HALO
    rows = []
    for c in range(C):
        total = wide[nb[c, 0] - start]
        for k in range(1, NB):
            total = total + wide[nb[c, k] - start]
        own = own_columns[c]
        rows.append(own + 0.5 * (0.25 * total - own))
    flat = jnp.concatenate(rows, axis=0)
    inv_rms = lax.rsqrt(jnp.mean(flat * flat, axis=1, keepdims=True) + 1e-05)
    normed = (flat * inv_rms * rows_in[L + 2:L + 3, 0:LEV]).astype(BF)
    which = which_ref[...]
    which4 = jnp.concatenate([which] * (FF // LEV), axis=1)
    pre = dot(normed, up[0])
    for e in range(1, E):
        pre = jnp.where(which4 == e, dot(normed, up[e]), pre)
    hidden = pre / (1.0 + jnp.exp(-pre))
    tendency = None
    for e in range(E):
        part = dot(jnp.where(which4 == e, hidden, 0.0).astype(BF), down[e])
        tendency = part if tendency is None else tendency + part
    out = flat + tendency
    picked = None
    for part in split3(out):
        got = dot(part, one_hot[...])
        picked = got if picked is None else picked + got
    place = place_in[...]
    sampled = jnp.zeros((MD, OBS), F32)
    for c in range(C):
        sampled = sampled + jnp.where(place == c, picked[c * MD:(c + 1) * MD, :], 0.0)
    sampled = sampled / rows_in[L + 1:L + 2, :]
    for g in range(GROUPS):
        for k in range(2):
            v_out[g, k] = sampled[:, k * LEV:(k + 1) * LEV]
            v_out[g, 2 + k] = out[(2 * g + k) * MD:(2 * g + k + 1) * MD]


def gram_kernel(values, at_obs, packed, centred):
    group = lax.axis_index("members")
    raw = jnp.concatenate([values[:, k].reshape(M, LEV) for k in range(2)], axis=1)
    mean = jnp.sum(raw, axis=0, keepdims=True) * (1.0 / M)
    pert = raw - mean
    again = jnp.sum(pert, axis=0, keepdims=True) * (1.0 / M)
    pert = pert - again
    centred[...] = pert
    innovation = at_obs[L:L + 1, :] - (mean + again)
    own = centred[pl.ds(pl.multiple_of(group * MD, MD), MD), :]
    w = at_obs[...]
    weights = [w[a:a + 1] * w[b:b + 1] * (1.0 / (L * M - 1)) for a, b in PAIRS]
    weights += [w[a:a + 1] * (1.0 / ROOT) for a in range(L)]
    left = jnp.concatenate([own * f for f in weights], axis=0)
    right = jnp.concatenate(
        [pert, jnp.broadcast_to(innovation, (M, OBS))], axis=0
    )
    lh, ll = split2(left)
    rh, rl = split2(right)
    s = dot_nt(lh, rh) + (dot_nt(lh, rl) + dot_nt(ll, rh))
    row = lax.broadcasted_iota(jnp.int32, (MD, M), 0) + group * MD
    column = lax.broadcasted_iota(jnp.int32, (MD, M), 1)
    for t in range(PACKS):
        first = s[(2 * t) * MD:(2 * t + 1) * MD, :M]
        second = s[(2 * t + 1) * MD:(2 * t + 2) * MD, :M]
        if t < L:
            k = len(PAIRS) + t
            middle = s[k * MD:(k + 1) * MD, M:]
        else:
            middle = jnp.zeros((MD, M), F32)
        p = jnp.where(column > row, first, jnp.where(column < row, second, middle))
        for h in range(2):
            for x in range(4):
                packed[2 * x + h, t] = p[8 * h:8 * h + 8]


def analysis_kernel(
    mine, other, values, modes, out,
    packed, crosses, zf, zh, fh,
):
    core = lax.axis_index("core")
    for g in range(GROUPS):
        for t in range(PACKS):
            at = pl.multiple_of(g * MD + core * 8, 8)
            packed[t, pl.ds(at, 8), :] = mine[g, t]
            at = pl.multiple_of(g * MD + 8 - core * 8, 8)
            packed[t, pl.ds(at, 8), :] = other[g, t]
    i = lax.broadcasted_iota(jnp.int32, (M, M), 0)
    j = lax.broadcasted_iota(jnp.int32, (M, M), 1)
    diagonal = i == j
    drives = []
    square = None
    for t in range(PACKS):
        p = packed[t]
        q = p.T
        if t < L:
            drives.append(jnp.sum(jnp.where(diagonal, p, 0.0), axis=0, keepdims=True))
        for side in range(2):
            keep = (i < j) if side == 0 else (i > j)
            s = jnp.where(diagonal, 0.0, jnp.where(keep, p, q))
            s = s - jnp.where(diagonal, jnp.sum(s, axis=0, keepdims=True), 0.0)
            k = 2 * t + side
            if k >= len(PAIRS):
                crosses[k - len(PAIRS)] = s
                continue
            a, b = PAIRS[k]
            if a == b:
                s = s + jnp.where(diagonal, 1.0, 0.0)
            zf[a * M:(a + 1) * M, b * M:(b + 1) * M] = s
            if a != b:
                zf[b * M:(b + 1) * M, a * M:(a + 1) * M] = s
            part = jnp.sum(s * s, axis=0, keepdims=True) * (1.0 if a == b else 2.0)
            square = part if square is None else square + part
    norm = jnp.sqrt(jnp.sum(square, axis=1, keepdims=True))
    inverse_norm = 1.0 / norm
    v = jnp.concatenate([drives[a] - 0.5 * crosses[a] for a in range(L)], axis=1)
    size = L * M
    z = zf[...] * inverse_norm
    for step in range(3):
        high, low = split2(z)
        zf[0:size] = z
        zh[0:size] = high
        zh[size:2 * size] = low
        vh, vl = split2(v)
        zh[2 * size:2 * size + M] = vh
        zh[2 * size + M:] = vl
        q = dot(zh[0:size], zh[0:size])
        fh[...] = (0.25 * q - 1.5 * zf[...]).astype(BF)
        if step == 2:
            new = dot(zh[2 * size:], fh[...])
            v = 2.25 * v + (new[:M] + new[M:])
            break
        new = dot(zh[...], fh[...])
        z = 2.25 * zf[...] + (new[0:size] + new[size:2 * size])
        v = 2.25 * v + (new[2 * size:2 * size + M] + new[2 * size + M:])
    for step in range(2):
        vh, vl = split2(v)
        got = dot(jnp.concatenate([vh, vl], axis=0), zh[0:size])
        got = got[:M] + (got[M:] + dot(vh, zh[size:2 * size]))
        th, tl = split2(got)
        new = dot(jnp.concatenate([th, tl], axis=0), fh[...])
        v = 1.5 * v - 0.5 * (2.25 * got + (new[:M] + new[M:]))
    v = v * inverse_norm
    blocks = []
    for a in range(L):
        block = v[:, a * M:(a + 1) * M]
        blocks.append(block - jnp.mean(block, axis=1, keepdims=True))
    coeff = jnp.concatenate(blocks, axis=0)
    ch, cl = split2(coeff)
    scaled = modes[...] * (1.0 / ROOT)
    columns = [values[:, 2 + k].reshape(M, LEV) for k in range(2)]
    bh, bl = split2(jnp.concatenate(columns, axis=1))
    r = dot(ch, bh) + (dot(cl, bh) + dot(ch, bl))
    for k in range(2):
        total = columns[k]
        for a in range(L):
            total = total + scaled[a:a + 1] * r[a * M:(a + 1) * M, k * LEV:(k + 1) * LEV]
        out[:, k] = total.reshape(GROUPS, MD, LEV)


def call(kernel, outs, scratch, total, smem=0, name=None):
    spaces = [pltpu.SMEM if n < smem else pltpu.VMEM for n in range(total)]
    return pl.pallas_call(
        kernel,
        out_shape=outs,
        in_specs=[pl.BlockSpec(memory_space=s) for s in spaces],
        out_specs=jax.tree.map(lambda _: pl.BlockSpec(memory_space=pltpu.VMEM), outs),
        scratch_shapes=scratch,
        compiler_params=pltpu.CompilerParams(vmem_limit_bytes=VMEM_LIMIT),
        name=name,
    )


def swap(x, axes):
    return lax.all_to_all(x, axes, split_axis=0, concat_axis=0, tiled=True)


def summed_copies(x, copies):
    total = jnp.sum(x, axis=0)
    return jnp.broadcast_to(total[None], (copies,) + total.shape)


def per_device(
    ensemble, neighbours, regime, norm_gain, up_weight, down_weight, vertical_modes,
    obs_col, obs_lev, obs_val, obs_err,
):
    shape = jax.ShapeDtypeStruct
    first = ensemble[:, :HALO, :]
    last = ensemble[:, C - HALO:, :]
    even = lax.axis_index("core") == 0
    apart = [(n, n + 1) for n in range(1, 63, 2)]
    outer = lax.ppermute(jnp.where(even, first, last), BANDS, apart + [(b, a) for a, b in apart])
    inner = lax.ppermute(jnp.where(even, last, first), "core", [(0, 1), (1, 0)])
    lev = obs_lev.reshape(1, OBS)
    col = obs_col.reshape(1, OBS)
    val = obs_val.reshape(1, OBS)
    err = obs_err.reshape(1, OBS)
    own, up, down, one_hot, which, at_obs, place = call(
        prepare_kernel,
        [
            shape((C, MD, LEV), F32), shape((E, LEV, FF), BF), shape((E, FF, LEV), BF),
            shape((LEV, OBS), BF), shape((C * MD, LEV), jnp.int32), shape((8, OBS), F32),
            shape((1, OBS), jnp.int32),
        ],
        [], 10, smem=1, name="prepare",
    )(
        regime, ensemble, up_weight, down_weight, col, lev, val, err, vertical_modes,
        norm_gain.reshape(1, LEV),
    )
    values = call(
        forecast_kernel,
        shape((GROUPS, 4, MD, LEV), F32),
        [pltpu.VMEM((C + 2 * HALO, MD, LEV), F32)],
        10, smem=1, name="forecast",
    )(neighbours, own, inner, outer, up, down, one_hot, which, at_obs, place)
    values = swap(values, "members")
    packed = call(
        gram_kernel,
        shape((8, PACKS, 8, M), F32),
        [pltpu.VMEM((M, OBS), F32)],
        2, name="gram",
    )(values, at_obs)
    packed = swap(packed, ("x", "core"))
    packed = swap(summed_copies(packed, 8), "z")
    mine = swap(summed_copies(packed, GROUPS), "members")
    other = lax.ppermute(mine, "core", [(0, 1), (1, 0)])
    size = L * M
    analysis = call(
        analysis_kernel,
        shape((GROUPS, 2, MD, LEV), F32),
        [
            pltpu.VMEM((PACKS, M, M), F32),
            pltpu.VMEM((L, M, M), F32),
            pltpu.VMEM((size, size), F32),
            pltpu.VMEM((2 * size + 2 * M, size), BF),
            pltpu.VMEM((size, size), BF),
        ],
        4, name="analysis",
    )(mine, other, values, vertical_modes)
    analysis = swap(analysis, "members")
    return analysis.transpose(2, 0, 1, 3).reshape(MD, C, LEV)


def solution(mesh):
    fine = Mesh(mesh.devices.reshape(8, 8, 4, 2), ("members",) + BANDS)
    in_specs = (
        P("members", BANDS, None),
        P(BANDS, None),
        P(BANDS),
        P(),
        P(),
        P(),
        P(),
        P(BANDS),
        P(BANDS),
        P(BANDS),
        P(BANDS),
    )
    out_specs = P("members", BANDS, None)
    return jax.shard_map(
        per_device, mesh=fine, in_specs=in_specs, out_specs=out_specs, check_vma=False
    )
```

```python
import functools
import math

import jax
import jax.numpy as jnp
from jax import lax
from jax.experimental import pallas as pl
from jax.experimental.pallas import tpu as pltpu
from jax.sharding import Mesh, PartitionSpec as P

E = 4
L = 4
NB = 4
HALO = 8
M = 128
LEV = 128
FF = 512
C = 16
MD = 16
OBS = 256
GROUPS = 8
PACKS = 7
PAIRS = [(a, b) for a in range(L) for b in range(a, L)]
ROOT = math.sqrt(L * M - 1)
BF = jnp.bfloat16
F32 = jnp.float32
VMEM_LIMIT = 40 * 1024 * 1024
BANDS = ("z", "x", "core")


def dot(a, b):
    return jnp.dot(a, b, preferred_element_type=F32)


def dot_nt(a, b):
    return lax.dot_general(a, b, (((1,), (1,)), ((), ())), preferred_element_type=F32)


def split2(a):
    high = a.astype(BF)
    return high, (a - high.astype(F32)).astype(BF)


def split3(a):
    high = a.astype(BF)
    rest = a - high.astype(F32)
    middle = rest.astype(BF)
    return high, middle, (rest - middle.astype(F32)).astype(BF)


def prepare_kernel(
    regime, ens, col, lev, val, err, modes, gain,
    own_out, hot_out, regs_out, w_out, place_out,
):
    band = (lax.axis_index("z") * 4 + lax.axis_index("x")) * 2 + lax.axis_index("core")
    place_out[...] = col[...] - band * C
    for c in range(C):
        own_out[c] = ens[:, c, :]
        regs_out[c * MD:(c + 1) * MD, :] = jnp.full((MD, LEV), regime[c], jnp.int32)
    one_hot = (lax.broadcasted_iota(jnp.int32, (LEV, OBS), 0) == lev[...]).astype(F32).astype(BF)
    hot_out[...] = one_hot
    at_obs = None
    for part in split3(modes[...]):
        got = dot(part, one_hot)
        at_obs = got if at_obs is None else at_obs + got
    w_out[0:L, :] = at_obs
    w_out[L:L + 1, :] = val[...] / err[...]
    w_out[L + 1:L + 2, :] = err[...]
    w_out[L + 2:L + 3, 0:LEV] = gain[...]


def forecast_kernel(
    nb, own_columns, inner, outer, up, down, one_hot, which_ref, rows_in, place_in,
    v_out, wide,
):
    core = lax.axis_index("core")
    band = (lax.axis_index("z") * 4 + lax.axis_index("x")) * 2 + core
    wide[HALO:HALO + C] = own_columns[...]
    inner_at = (1 - core) * (HALO + C)
    outer_at = core * (HALO + C)
    for c in range(HALO):
        wide[inner_at + c] = inner[:, c, :]
        wide[outer_at + c] = outer[:, c, :]
    start = band * C - HALO
    rows = []
    for c in range(C):
        total = wide[nb[c, 0] - start]
        for k in range(1, NB):
            total = total + wide[nb[c, k] - start]
        own = own_columns[c]
        rows.append(own + 0.5 * (0.25 * total - own))
    flat = jnp.concatenate(rows, axis=0)
    inv_rms = lax.rsqrt(jnp.mean(flat * flat, axis=1, keepdims=True) + 1e-05)
    normed = (flat * inv_rms * rows_in[L + 2:L + 3, 0:LEV]).astype(BF)
    which = which_ref[...]
    which4 = jnp.concatenate([which] * (FF // LEV), axis=1)
    pre = dot(normed, up[0])
    for e in range(1, E):
        pre = jnp.where(which4 == e, dot(normed, up[e]), pre)
    hidden = pre / (1.0 + jnp.exp(-pre))
    tendency = None
    for e in range(E):
        part = dot(jnp.where(which4 == e, hidden, 0.0).astype(BF), down[e])
        tendency = part if tendency is None else tendency + part
    out = flat + tendency
    picked = None
    for part in split3(out):
        got = dot(part, one_hot[...])
        picked = got if picked is None else picked + got
    place = place_in[...]
    sampled = jnp.zeros((MD, OBS), F32)
    for c in range(C):
        sampled = sampled + jnp.where(place == c, picked[c * MD:(c + 1) * MD, :], 0.0)
    sampled = sampled / rows_in[L + 1:L + 2, :]
    for g in range(GROUPS):
        for k in range(2):
            v_out[g, k] = sampled[:, k * LEV:(k + 1) * LEV]
            v_out[g, 2 + k] = out[(2 * g + k) * MD:(2 * g + k + 1) * MD]


def gram_kernel(values, at_obs, packed, centred):
    group = lax.axis_index("members")
    raw = jnp.concatenate([values[:, k].reshape(M, LEV) for k in range(2)], axis=1)
    mean = jnp.sum(raw, axis=0, keepdims=True) * (1.0 / M)
    pert = raw - mean
    again = jnp.sum(pert, axis=0, keepdims=True) * (1.0 / M)
    pert = pert - again
    centred[...] = pert
    innovation = at_obs[L:L + 1, :] - (mean + again)
    own = centred[pl.ds(pl.multiple_of(group * MD, MD), MD), :]
    w = at_obs[...]
    weights = [w[a:a + 1] * w[b:b + 1] * (1.0 / (L * M - 1)) for a, b in PAIRS]
    weights += [w[a:a + 1] * (1.0 / ROOT) for a in range(L)]
    left = jnp.concatenate([own * f for f in weights], axis=0)
    right = jnp.concatenate(
        [pert, jnp.broadcast_to(innovation, (M, OBS))], axis=0
    )
    lh, ll = split2(left)
    rh, rl = split2(right)
    s = dot_nt(lh, rh) + (dot_nt(lh, rl) + dot_nt(ll, rh))
    row = lax.broadcasted_iota(jnp.int32, (MD, M), 0) + group * MD
    column = lax.broadcasted_iota(jnp.int32, (MD, M), 1)
    for t in range(PACKS):
        first = s[(2 * t) * MD:(2 * t + 1) * MD, :M]
        second = s[(2 * t + 1) * MD:(2 * t + 2) * MD, :M]
        if t < L:
            k = len(PAIRS) + t
            middle = s[k * MD:(k + 1) * MD, M:]
        else:
            middle = jnp.zeros((MD, M), F32)
        p = jnp.where(column > row, first, jnp.where(column < row, second, middle))
        for h in range(2):
            for x in range(4):
                packed[2 * x + h, t] = p[8 * h:8 * h + 8]


def analysis_kernel(
    mine, other, values, modes, out,
    packed, crosses, zf, zh, fh,
):
    core = lax.axis_index("core")
    for g in range(GROUPS):
        for t in range(PACKS):
            at = pl.multiple_of(g * MD + core * 8, 8)
            packed[t, pl.ds(at, 8), :] = mine[g, t]
            at = pl.multiple_of(g * MD + 8 - core * 8, 8)
            packed[t, pl.ds(at, 8), :] = other[g, t]
    i = lax.broadcasted_iota(jnp.int32, (M, M), 0)
    j = lax.broadcasted_iota(jnp.int32, (M, M), 1)
    diagonal = i == j
    drives = []
    square = None
    for t in range(PACKS):
        p = packed[t]
        q = p.T
        if t < L:
            drives.append(jnp.sum(jnp.where(diagonal, p, 0.0), axis=0, keepdims=True))
        for side in range(2):
            keep = (i < j) if side == 0 else (i > j)
            s = jnp.where(diagonal, 0.0, jnp.where(keep, p, q))
            s = s - jnp.where(diagonal, jnp.sum(s, axis=0, keepdims=True), 0.0)
            k = 2 * t + side
            if k >= len(PAIRS):
                crosses[k - len(PAIRS)] = s
                continue
            a, b = PAIRS[k]
            if a == b:
                s = s + jnp.where(diagonal, 1.0, 0.0)
            zf[a * M:(a + 1) * M, b * M:(b + 1) * M] = s
            if a != b:
                zf[b * M:(b + 1) * M, a * M:(a + 1) * M] = s
            part = jnp.sum(s * s, axis=0, keepdims=True) * (1.0 if a == b else 2.0)
            square = part if square is None else square + part
    norm = jnp.sqrt(jnp.sum(square, axis=1, keepdims=True))
    inverse_norm = 1.0 / norm
    v = jnp.concatenate([drives[a] - 0.5 * crosses[a] for a in range(L)], axis=1)
    size = L * M
    z = zf[...] * inverse_norm
    for step in range(3):
        high, low = split2(z)
        zf[0:size] = z
        zh[0:size] = high
        zh[size:2 * size] = low
        vh, vl = split2(v)
        zh[2 * size:2 * size + M] = vh
        zh[2 * size + M:] = vl
        q = dot(zh[0:size], zh[0:size])
        fh[...] = (0.25 * q - 1.5 * zf[...]).astype(BF)
        if step == 2:
            new = dot(zh[2 * size:], fh[...])
            v = 2.25 * v + (new[:M] + new[M:])
            break
        new = dot(zh[...], fh[...])
        z = 2.25 * zf[...] + (new[0:size] + new[size:2 * size])
        v = 2.25 * v + (new[2 * size:2 * size + M] + new[2 * size + M:])
    for step in range(2):
        vh, vl = split2(v)
        got = dot(jnp.concatenate([vh, vl], axis=0), zh[0:size])
        got = got[:M] + (got[M:] + dot(vh, zh[size:2 * size]))
        th, tl = split2(got)
        new = dot(jnp.concatenate([th, tl], axis=0), fh[...])
        v = 1.5 * v - 0.5 * (2.25 * got + (new[:M] + new[M:]))
    v = v * inverse_norm
    blocks = []
    for a in range(L):
        block = v[:, a * M:(a + 1) * M]
        blocks.append(block - jnp.mean(block, axis=1, keepdims=True))
    coeff = jnp.concatenate(blocks, axis=0)
    ch, cl = split2(coeff)
    scaled = modes[...] * (1.0 / ROOT)
    columns = [values[:, 2 + k].reshape(M, LEV) for k in range(2)]
    bh, bl = split2(jnp.concatenate(columns, axis=1))
    r = dot(ch, bh) + (dot(cl, bh) + dot(ch, bl))
    for k in range(2):
        total = columns[k]
        for a in range(L):
            total = total + scaled[a:a + 1] * r[a * M:(a + 1) * M, k * LEV:(k + 1) * LEV]
        out[:, k] = total.reshape(GROUPS, MD, LEV)


def call(kernel, outs, scratch, total, smem=0, name=None, cost=None):
    spaces = [pltpu.SMEM if n < smem else pltpu.VMEM for n in range(total)]
    return pl.pallas_call(
        kernel,
        out_shape=outs,
        in_specs=[pl.BlockSpec(memory_space=s) for s in spaces],
        out_specs=jax.tree.map(lambda _: pl.BlockSpec(memory_space=pltpu.VMEM), outs),
        scratch_shapes=scratch,
        compiler_params=pltpu.CompilerParams(vmem_limit_bytes=VMEM_LIMIT),
        name=name,
        cost_estimate=cost,
    )


def swap(x, axes):
    return lax.all_to_all(x, axes, split_axis=0, concat_axis=0, tiled=True)


def summed_copies(x, copies):
    total = jnp.sum(x, axis=0)
    return jnp.broadcast_to(total[None], (copies,) + total.shape)


def per_device(
    ensemble, neighbours, regime, norm_gain, up_weight, down_weight, vertical_modes,
    obs_col, obs_lev, obs_val, obs_err,
):
    shape = jax.ShapeDtypeStruct
    first = ensemble[:, :HALO, :]
    last = ensemble[:, C - HALO:, :]
    even = lax.axis_index("core") == 0
    apart = [(n, n + 1) for n in range(1, 63, 2)]
    outer = lax.ppermute(jnp.where(even, first, last), BANDS, apart + [(b, a) for a, b in apart])
    inner = lax.ppermute(jnp.where(even, last, first), "core", [(0, 1), (1, 0)])
    lev = obs_lev.reshape(1, OBS)
    col = obs_col.reshape(1, OBS)
    val = obs_val.reshape(1, OBS)
    err = obs_err.reshape(1, OBS)
    own, one_hot, which, at_obs, place = call(
        prepare_kernel,
        [
            shape((C, MD, LEV), F32), shape((LEV, OBS), BF), shape((C * MD, LEV), jnp.int32), shape((8, OBS), F32),
            shape((1, OBS), jnp.int32),
        ],
        [], 8, smem=1, name="prepare", cost=pl.CostEstimate(flops=1 << 33, bytes_accessed=1 << 20, transcendentals=0),
    )(
        regime, ensemble, col, lev, val, err, vertical_modes,
        norm_gain.reshape(1, LEV),
    )
    values = call(
        forecast_kernel,
        shape((GROUPS, 4, MD, LEV), F32),
        [pltpu.VMEM((C + 2 * HALO, MD, LEV), F32)],
        10, smem=1, name="forecast",
    )(neighbours, own, inner, outer, up_weight, down_weight, one_hot, which, at_obs, place)
    values = swap(values, "members")
    packed = call(
        gram_kernel,
        shape((8, PACKS, 8, M), F32),
        [pltpu.VMEM((M, OBS), F32)],
        2, name="gram",
    )(values, at_obs)
    packed = swap(packed, ("x", "core"))
    packed = swap(summed_copies(packed, 8), "z")
    mine = swap(summed_copies(packed, GROUPS), "members")
    other = lax.ppermute(mine, "core", [(0, 1), (1, 0)])
    size = L * M
    analysis = call(
        analysis_kernel,
        shape((GROUPS, 2, MD, LEV), F32),
        [
            pltpu.VMEM((PACKS, M, M), F32),
            pltpu.VMEM((L, M, M), F32),
            pltpu.VMEM((size, size), F32),
            pltpu.VMEM((2 * size + 2 * M, size), BF),
            pltpu.VMEM((size, size), BF),
        ],
        4, name="analysis",
    )(mine, other, values, vertical_modes)
    analysis = swap(analysis, "members")
    return analysis.transpose(2, 0, 1, 3).reshape(MD, C, LEV)


def solution(mesh):
    fine = Mesh(mesh.devices.reshape(8, 8, 4, 2), ("members",) + BANDS)
    in_specs = (
        P("members", BANDS, None),
        P(BANDS, None),
        P(BANDS),
        P(),
        P(),
        P(),
        P(),
        P(BANDS),
        P(BANDS),
        P(BANDS),
        P(BANDS),
    )
    out_specs = P("members", BANDS, None)
    return jax.shard_map(
        per_device, mesh=fine, in_specs=in_specs, out_specs=out_specs, check_vma=False
    )
```

```python
import functools
import math

import jax
import jax.numpy as jnp
from jax import lax
from jax.experimental import pallas as pl
from jax.experimental.pallas import tpu as pltpu
from jax.sharding import Mesh, PartitionSpec as P

E = 4
L = 4
NB = 4
HALO = 8
M = 128
LEV = 128
FF = 512
C = 16
MD = 16
OBS = 256
GROUPS = 8
PACKS = 7
PAIRS = [(a, b) for a in range(L) for b in range(a, L)]
ROOT = math.sqrt(L * M - 1)
BF = jnp.bfloat16
F32 = jnp.float32
VMEM_LIMIT = 40 * 1024 * 1024
BANDS = ("z", "x", "core")


def dot(a, b):
    return jnp.dot(a, b, preferred_element_type=F32)


def dot_nt(a, b):
    return lax.dot_general(a, b, (((1,), (1,)), ((), ())), preferred_element_type=F32)


def split2(a):
    high = a.astype(BF)
    return high, (a - high.astype(F32)).astype(BF)


def split3(a):
    high = a.astype(BF)
    rest = a - high.astype(F32)
    middle = rest.astype(BF)
    return high, middle, (rest - middle.astype(F32)).astype(BF)


def prepare_kernel(
    regime, col, lev, val, err, modes, gain,
    hot_out, regs_out, w_out, place_out,
):
    band = (lax.axis_index("z") * 4 + lax.axis_index("x")) * 2 + lax.axis_index("core")
    place_out[...] = col[...] - band * C
    for c in range(C):
        regs_out[c * MD:(c + 1) * MD, :] = jnp.full((MD, LEV), regime[c], jnp.int32)
    one_hot = (lax.broadcasted_iota(jnp.int32, (LEV, OBS), 0) == lev[...]).astype(F32).astype(BF)
    hot_out[...] = one_hot
    at_obs = None
    for part in split3(modes[...]):
        got = dot(part, one_hot)
        at_obs = got if at_obs is None else at_obs + got
    w_out[0:L, :] = at_obs
    w_out[L:L + 1, :] = val[...] / err[...]
    w_out[L + 1:L + 2, :] = err[...]
    w_out[L + 2:L + 3, 0:LEV] = gain[...]


def forecast_kernel(
    nb, ens, inner, outer, up, down, one_hot, which_ref, rows_in, place_in,
    v_out, wide, halves,
):
    core = lax.axis_index("core")
    band = (lax.axis_index("z") * 4 + lax.axis_index("x")) * 2 + core
    for c in range(C):
        wide[HALO + c] = ens[:, c, :]
    inner_at = (1 - core) * (HALO + C)
    outer_at = core * (HALO + C)
    halves[0] = inner[:, pl.ds(pl.multiple_of(core * HALO, HALO), HALO), :]
    halves[1] = outer[:, pl.ds(pl.multiple_of((1 - core) * HALO, HALO), HALO), :]
    for c in range(HALO):
        wide[inner_at + c] = halves[0, :, c, :]
        wide[outer_at + c] = halves[1, :, c, :]
    start = band * C - HALO
    rows = []
    for c in range(C):
        total = wide[nb[c, 0] - start]
        for k in range(1, NB):
            total = total + wide[nb[c, k] - start]
        own = wide[HALO + c]
        rows.append(own + 0.5 * (0.25 * total - own))
    flat = jnp.concatenate(rows, axis=0)
    inv_rms = lax.rsqrt(jnp.mean(flat * flat, axis=1, keepdims=True) + 1e-05)
    normed = (flat * inv_rms * rows_in[L + 2:L + 3, 0:LEV]).astype(BF)
    which = which_ref[...]
    which4 = jnp.concatenate([which] * (FF // LEV), axis=1)
    pre = dot(normed, up[0])
    for e in range(1, E):
        pre = jnp.where(which4 == e, dot(normed, up[e]), pre)
    hidden = pre / (1.0 + jnp.exp(-pre))
    tendency = None
    for e in range(E):
        part = dot(jnp.where(which4 == e, hidden, 0.0).astype(BF), down[e])
        tendency = part if tendency is None else tendency + part
    out = flat + tendency
    picked = None
    for part in split3(out):
        got = dot(part, one_hot[...])
        picked = got if picked is None else picked + got
    place = place_in[...]
    sampled = jnp.zeros((MD, OBS), F32)
    for c in range(C):
        sampled = sampled + jnp.where(place == c, picked[c * MD:(c + 1) * MD, :], 0.0)
    sampled = sampled / rows_in[L + 1:L + 2, :]
    for g in range(GROUPS):
        for k in range(2):
            v_out[g, k] = sampled[:, k * LEV:(k + 1) * LEV]
            v_out[g, 2 + k] = out[(2 * g + k) * MD:(2 * g + k + 1) * MD]


def gram_kernel(values, at_obs, packed, centred):
    group = lax.axis_index("members")
    raw = jnp.concatenate([values[:, k].reshape(M, LEV) for k in range(2)], axis=1)
    mean = jnp.sum(raw, axis=0, keepdims=True) * (1.0 / M)
    pert = raw - mean
    again = jnp.sum(pert, axis=0, keepdims=True) * (1.0 / M)
    pert = pert - again
    centred[...] = pert
    innovation = at_obs[L:L + 1, :] - (mean + again)
    own = centred[pl.ds(pl.multiple_of(group * MD, MD), MD), :]
    w = at_obs[...]
    weights = [w[a:a + 1] * w[b:b + 1] * (1.0 / (L * M - 1)) for a, b in PAIRS]
    weights += [w[a:a + 1] * (1.0 / ROOT) for a in range(L)]
    left = jnp.concatenate([own * f for f in weights], axis=0)
    right = jnp.concatenate(
        [pert, jnp.broadcast_to(innovation, (M, OBS))], axis=0
    )
    lh, ll = split2(left)
    rh, rl = split2(right)
    s = dot_nt(lh, rh) + (dot_nt(lh, rl) + dot_nt(ll, rh))
    row = lax.broadcasted_iota(jnp.int32, (MD, M), 0) + group * MD
    column = lax.broadcasted_iota(jnp.int32, (MD, M), 1)
    for t in range(PACKS):
        first = s[(2 * t) * MD:(2 * t + 1) * MD, :M]
        second = s[(2 * t + 1) * MD:(2 * t + 2) * MD, :M]
        if t < L:
            k = len(PAIRS) + t
            middle = s[k * MD:(k + 1) * MD, M:]
        else:
            middle = jnp.zeros((MD, M), F32)
        p = jnp.where(column > row, first, jnp.where(column < row, second, middle))
        for h in range(2):
            for x in range(4):
                packed[2 * x + h, t] = p[8 * h:8 * h + 8]


def analysis_kernel(
    mine, other, values, modes, out,
    packed, crosses, zf, zh, fh,
):
    core = lax.axis_index("core")
    for g in range(GROUPS):
        for t in range(PACKS):
            at = pl.multiple_of(g * MD + core * 8, 8)
            packed[t, pl.ds(at, 8), :] = mine[g, t]
            at = pl.multiple_of(g * MD + 8 - core * 8, 8)
            packed[t, pl.ds(at, 8), :] = other[g, t]
    i = lax.broadcasted_iota(jnp.int32, (M, M), 0)
    j = lax.broadcasted_iota(jnp.int32, (M, M), 1)
    diagonal = i == j
    drives = []
    square = None
    for t in range(PACKS):
        p = packed[t]
        q = p.T
        if t < L:
            drives.append(jnp.sum(jnp.where(diagonal, p, 0.0), axis=0, keepdims=True))
        for side in range(2):
            keep = (i < j) if side == 0 else (i > j)
            s = jnp.where(diagonal, 0.0, jnp.where(keep, p, q))
            s = s - jnp.where(diagonal, jnp.sum(s, axis=0, keepdims=True), 0.0)
            k = 2 * t + side
            if k >= len(PAIRS):
                crosses[k - len(PAIRS)] = s
                continue
            a, b = PAIRS[k]
            if a == b:
                s = s + jnp.where(diagonal, 1.0, 0.0)
            zf[a * M:(a + 1) * M, b * M:(b + 1) * M] = s
            if a != b:
                zf[b * M:(b + 1) * M, a * M:(a + 1) * M] = s
            part = jnp.sum(s * s, axis=0, keepdims=True) * (1.0 if a == b else 2.0)
            square = part if square is None else square + part
    norm = jnp.sqrt(jnp.sum(square, axis=1, keepdims=True))
    inverse_norm = 1.0 / norm
    v = jnp.concatenate([drives[a] - 0.5 * crosses[a] for a in range(L)], axis=1)
    size = L * M
    z = zf[...] * inverse_norm
    for step in range(3):
        high, low = split2(z)
        zf[0:size] = z
        zh[0:size] = high
        zh[size:2 * size] = low
        vh, vl = split2(v)
        zh[2 * size:2 * size + M] = vh
        zh[2 * size + M:] = vl
        q = dot(zh[0:size], zh[0:size])
        fh[...] = (0.25 * q - 1.5 * zf[...]).astype(BF)
        if step == 2:
            new = dot(zh[2 * size:], fh[...])
            v = 2.25 * v + (new[:M] + new[M:])
            break
        new = dot(zh[...], fh[...])
        z = 2.25 * zf[...] + (new[0:size] + new[size:2 * size])
        v = 2.25 * v + (new[2 * size:2 * size + M] + new[2 * size + M:])
    for step in range(2):
        vh, vl = split2(v)
        got = dot(jnp.concatenate([vh, vl], axis=0), zh[0:size])
        got = got[:M] + (got[M:] + dot(vh, zh[size:2 * size]))
        th, tl = split2(got)
        new = dot(jnp.concatenate([th, tl], axis=0), fh[...])
        v = 1.5 * v - 0.5 * (2.25 * got + (new[:M] + new[M:]))
    v = v * inverse_norm
    blocks = []
    for a in range(L):
        block = v[:, a * M:(a + 1) * M]
        blocks.append(block - jnp.mean(block, axis=1, keepdims=True))
    coeff = jnp.concatenate(blocks, axis=0)
    ch, cl = split2(coeff)
    scaled = modes[...] * (1.0 / ROOT)
    columns = [values[:, 2 + k].reshape(M, LEV) for k in range(2)]
    bh, bl = split2(jnp.concatenate(columns, axis=1))
    r = dot(ch, bh) + (dot(cl, bh) + dot(ch, bl))
    for k in range(2):
        total = columns[k]
        for a in range(L):
            total = total + scaled[a:a + 1] * r[a * M:(a + 1) * M, k * LEV:(k + 1) * LEV]
        out[:, k] = total.reshape(GROUPS, MD, LEV)


def call(kernel, outs, scratch, total, smem=0, name=None, cost=None):
    spaces = [pltpu.SMEM if n < smem else pltpu.VMEM for n in range(total)]
    return pl.pallas_call(
        kernel,
        out_shape=outs,
        in_specs=[pl.BlockSpec(memory_space=s) for s in spaces],
        out_specs=jax.tree.map(lambda _: pl.BlockSpec(memory_space=pltpu.VMEM), outs),
        scratch_shapes=scratch,
        compiler_params=pltpu.CompilerParams(vmem_limit_bytes=VMEM_LIMIT),
        name=name,
        cost_estimate=cost,
    )


def swap(x, axes):
    return lax.all_to_all(x, axes, split_axis=0, concat_axis=0, tiled=True)


def summed_copies(x, copies):
    total = jnp.sum(x, axis=0)
    return jnp.broadcast_to(total[None], (copies,) + total.shape)


def per_device(
    ensemble, neighbours, regime, norm_gain, up_weight, down_weight, vertical_modes,
    obs_col, obs_lev, obs_val, obs_err,
):
    shape = jax.ShapeDtypeStruct
    apart = [(n, n + 1) for n in range(1, 63, 2)]
    outer = lax.ppermute(ensemble, BANDS, apart + [(b, a) for a, b in apart])
    inner = lax.ppermute(ensemble, "core", [(0, 1), (1, 0)])
    lev = obs_lev.reshape(1, OBS)
    col = obs_col.reshape(1, OBS)
    val = obs_val.reshape(1, OBS)
    err = obs_err.reshape(1, OBS)
    one_hot, which, at_obs, place = call(
        prepare_kernel,
        [
            shape((LEV, OBS), BF), shape((C * MD, LEV), jnp.int32), shape((8, OBS), F32),
            shape((1, OBS), jnp.int32),
        ],
        [], 7, smem=1, name="prepare", cost=pl.CostEstimate(flops=1 << 33, bytes_accessed=1 << 20, transcendentals=0),
    )(
        regime, col, lev, val, err, vertical_modes,
        norm_gain.reshape(1, LEV),
    )
    values = call(
        forecast_kernel,
        shape((GROUPS, 4, MD, LEV), F32),
        [pltpu.VMEM((C + 2 * HALO, MD, LEV), F32), pltpu.VMEM((2, MD, HALO, LEV), F32)],
        10, smem=1, name="forecast",
    )(neighbours, ensemble, inner, outer, up_weight, down_weight, one_hot, which, at_obs, place)
    values = swap(values, "members")
    packed = call(
        gram_kernel,
        shape((8, PACKS, 8, M), F32),
        [pltpu.VMEM((M, OBS), F32)],
        2, name="gram",
    )(values, at_obs)
    packed = swap(packed, ("x", "core"))
    packed = swap(summed_copies(packed, 8), "z")
    mine = swap(summed_copies(packed, GROUPS), "members")
    other = lax.ppermute(mine, "core", [(0, 1), (1, 0)])
    size = L * M
    analysis = call(
        analysis_kernel,
        shape((GROUPS, 2, MD, LEV), F32),
        [
            pltpu.VMEM((PACKS, M, M), F32),
            pltpu.VMEM((L, M, M), F32),
            pltpu.VMEM((size, size), F32),
            pltpu.VMEM((2 * size + 2 * M, size), BF),
            pltpu.VMEM((size, size), BF),
        ],
        4, name="analysis",
    )(mine, other, values, vertical_modes)
    analysis = swap(analysis, "members")
    return analysis.transpose(2, 0, 1, 3).reshape(MD, C, LEV)


def solution(mesh):
    fine = Mesh(mesh.devices.reshape(8, 8, 4, 2), ("members",) + BANDS)
    in_specs = (
        P("members", BANDS, None),
        P(BANDS, None),
        P(BANDS),
        P(),
        P(),
        P(),
        P(),
        P(BANDS),
        P(BANDS),
        P(BANDS),
        P(BANDS),
    )
    out_specs = P("members", BANDS, None)
    return jax.shard_map(
        per_device, mesh=fine, in_specs=in_specs, out_specs=out_specs, check_vma=False
    )
```

```python
import functools
import math

import jax
import jax.numpy as jnp
from jax import lax
from jax.experimental import pallas as pl
from jax.experimental.pallas import tpu as pltpu
from jax.sharding import Mesh, PartitionSpec as P

E = 4
L = 4
NB = 4
HALO = 8
M = 128
LEV = 128
FF = 512
C = 16
MD = 16
OBS = 256
GROUPS = 8
PACKS = 7
PAIRS = [(a, b) for a in range(L) for b in range(a, L)]
ROOT = math.sqrt(L * M - 1)
BF = jnp.bfloat16
F32 = jnp.float32
VMEM_LIMIT = 40 * 1024 * 1024
BANDS = ("z", "x", "core")


def dot(a, b):
    return jnp.dot(a, b, preferred_element_type=F32)


def dot_nt(a, b):
    return lax.dot_general(a, b, (((1,), (1,)), ((), ())), preferred_element_type=F32)


def split2(a):
    high = a.astype(BF)
    return high, (a - high.astype(F32)).astype(BF)


def split3(a):
    high = a.astype(BF)
    rest = a - high.astype(F32)
    middle = rest.astype(BF)
    return high, middle, (rest - middle.astype(F32)).astype(BF)


def prepare_kernel(
    regime, col, lev, val, err, modes, gain,
    hot_out, regs_out, w_out, place_out,
):
    band = (lax.axis_index("z") * 4 + lax.axis_index("x")) * 2 + lax.axis_index("core")
    place_out[...] = col[...] - band * C
    for c in range(C):
        regs_out[c * MD:(c + 1) * MD, :] = jnp.full((MD, LEV), regime[c], jnp.int32)
    one_hot = (lax.broadcasted_iota(jnp.int32, (LEV, OBS), 0) == lev[...]).astype(F32).astype(BF)
    hot_out[...] = one_hot
    at_obs = None
    for part in split3(modes[...]):
        got = dot(part, one_hot)
        at_obs = got if at_obs is None else at_obs + got
    w_out[0:L, :] = at_obs
    w_out[L:L + 1, :] = val[...] / err[...]
    w_out[L + 1:L + 2, :] = err[...]
    w_out[L + 2:L + 3, 0:LEV] = gain[...]


def forecast_kernel(
    nb, ens, outer, inner, up, down, one_hot, which_ref, rows_in, place_in,
    v_out, wide, halves,
):
    core = lax.axis_index("core")
    band = (lax.axis_index("z") * 4 + lax.axis_index("x")) * 2 + core
    for c in range(C):
        wide[HALO + c] = ens[:, c, :]
    inner_at = (1 - core) * (HALO + C)
    outer_at = core * (HALO + C)
    halves[0] = inner[:, pl.ds(pl.multiple_of(core * HALO, HALO), HALO), :]
    halves[1] = outer[:, pl.ds(pl.multiple_of((1 - core) * HALO, HALO), HALO), :]
    for c in range(HALO):
        wide[inner_at + c] = halves[0, :, c, :]
        wide[outer_at + c] = halves[1, :, c, :]
    start = band * C - HALO
    rows = []
    for c in range(C):
        total = wide[nb[c, 0] - start]
        for k in range(1, NB):
            total = total + wide[nb[c, k] - start]
        own = wide[HALO + c]
        rows.append(own + 0.5 * (0.25 * total - own))
    flat = jnp.concatenate(rows, axis=0)
    inv_rms = lax.rsqrt(jnp.mean(flat * flat, axis=1, keepdims=True) + 1e-05)
    normed = (flat * inv_rms * rows_in[L + 2:L + 3, 0:LEV]).astype(BF)
    which = which_ref[...]
    which4 = jnp.concatenate([which] * (FF // LEV), axis=1)
    pre = dot(normed, up[0])
    for e in range(1, E):
        pre = jnp.where(which4 == e, dot(normed, up[e]), pre)
    hidden = pre / (1.0 + jnp.exp(-pre))
    tendency = None
    for e in range(E):
        part = dot(jnp.where(which4 == e, hidden, 0.0).astype(BF), down[e])
        tendency = part if tendency is None else tendency + part
    out = flat + tendency
    picked = None
    for part in split3(out):
        got = dot(part, one_hot[...])
        picked = got if picked is None else picked + got
    place = place_in[...]
    sampled = jnp.zeros((MD, OBS), F32)
    for c in range(C):
        sampled = sampled + jnp.where(place == c, picked[c * MD:(c + 1) * MD, :], 0.0)
    sampled = sampled / rows_in[L + 1:L + 2, :]
    for g in range(GROUPS):
        for k in range(2):
            v_out[g, k] = sampled[:, k * LEV:(k + 1) * LEV]
            v_out[g, 2 + k] = out[(2 * g + k) * MD:(2 * g + k + 1) * MD]


def gram_kernel(values, at_obs, packed, centred):
    group = lax.axis_index("members")
    raw = jnp.concatenate([values[:, k].reshape(M, LEV) for k in range(2)], axis=1)
    mean = jnp.sum(raw, axis=0, keepdims=True) * (1.0 / M)
    pert = raw - mean
    again = jnp.sum(pert, axis=0, keepdims=True) * (1.0 / M)
    pert = pert - again
    centred[...] = pert
    innovation = at_obs[L:L + 1, :] - (mean + again)
    own = centred[pl.ds(pl.multiple_of(group * MD, MD), MD), :]
    w = at_obs[...]
    weights = [w[a:a + 1] * w[b:b + 1] * (1.0 / (L * M - 1)) for a, b in PAIRS]
    weights += [w[a:a + 1] * (1.0 / ROOT) for a in range(L)]
    left = jnp.concatenate([own * f for f in weights], axis=0)
    right = jnp.concatenate(
        [pert, jnp.broadcast_to(innovation, (M, OBS))], axis=0
    )
    lh, ll = split2(left)
    rh, rl = split2(right)
    s = dot_nt(lh, rh) + (dot_nt(lh, rl) + dot_nt(ll, rh))
    row = lax.broadcasted_iota(jnp.int32, (MD, M), 0) + group * MD
    column = lax.broadcasted_iota(jnp.int32, (MD, M), 1)
    for t in range(PACKS):
        first = s[(2 * t) * MD:(2 * t + 1) * MD, :M]
        second = s[(2 * t + 1) * MD:(2 * t + 2) * MD, :M]
        if t < L:
            k = len(PAIRS) + t
            middle = s[k * MD:(k + 1) * MD, M:]
        else:
            middle = jnp.zeros((MD, M), F32)
        p = jnp.where(column > row, first, jnp.where(column < row, second, middle))
        for h in range(2):
            for x in range(4):
                packed[2 * x + h, t] = p[8 * h:8 * h + 8]


def analysis_kernel(
    mine, other, values, modes, out,
    packed, crosses, zf, zh, fh,
):
    core = lax.axis_index("core")
    for g in range(GROUPS):
        for t in range(PACKS):
            at = pl.multiple_of(g * MD + core * 8, 8)
            packed[t, pl.ds(at, 8), :] = mine[g, t]
            at = pl.multiple_of(g * MD + 8 - core * 8, 8)
            packed[t, pl.ds(at, 8), :] = other[g, t]
    i = lax.broadcasted_iota(jnp.int32, (M, M), 0)
    j = lax.broadcasted_iota(jnp.int32, (M, M), 1)
    diagonal = i == j
    drives = []
    square = None
    for t in range(PACKS):
        p = packed[t]
        q = p.T
        if t < L:
            drives.append(jnp.sum(jnp.where(diagonal, p, 0.0), axis=0, keepdims=True))
        for side in range(2):
            keep = (i < j) if side == 0 else (i > j)
            s = jnp.where(diagonal, 0.0, jnp.where(keep, p, q))
            s = s - jnp.where(diagonal, jnp.sum(s, axis=0, keepdims=True), 0.0)
            k = 2 * t + side
            if k >= len(PAIRS):
                crosses[k - len(PAIRS)] = s
                continue
            a, b = PAIRS[k]
            if a == b:
                s = s + jnp.where(diagonal, 1.0, 0.0)
            zf[a * M:(a + 1) * M, b * M:(b + 1) * M] = s
            if a != b:
                zf[b * M:(b + 1) * M, a * M:(a + 1) * M] = s
            part = jnp.sum(s * s, axis=0, keepdims=True) * (1.0 if a == b else 2.0)
            square = part if square is None else square + part
    norm = jnp.sqrt(jnp.sum(square, axis=1, keepdims=True))
    inverse_norm = 1.0 / norm
    v = jnp.concatenate([drives[a] - 0.5 * crosses[a] for a in range(L)], axis=1)
    size = L * M
    z = zf[...] * inverse_norm
    for step in range(3):
        high, low = split2(z)
        zf[0:size] = z
        zh[0:size] = high
        zh[size:2 * size] = low
        vh, vl = split2(v)
        zh[2 * size:2 * size + M] = vh
        zh[2 * size + M:] = vl
        q = dot(zh[0:size], zh[0:size])
        fh[...] = (0.25 * q - 1.5 * zf[...]).astype(BF)
        if step == 2:
            new = dot(zh[2 * size:], fh[...])
            v = 2.25 * v + (new[:M] + new[M:])
            break
        new = dot(zh[...], fh[...])
        z = 2.25 * zf[...] + (new[0:size] + new[size:2 * size])
        v = 2.25 * v + (new[2 * size:2 * size + M] + new[2 * size + M:])
    for step in range(2):
        vh, vl = split2(v)
        got = dot(jnp.concatenate([vh, vl], axis=0), zh[0:size])
        got = got[:M] + (got[M:] + dot(vh, zh[size:2 * size]))
        th, tl = split2(got)
        new = dot(jnp.concatenate([th, tl], axis=0), fh[...])
        v = 1.5 * v - 0.5 * (2.25 * got + (new[:M] + new[M:]))
    v = v * inverse_norm
    blocks = []
    for a in range(L):
        block = v[:, a * M:(a + 1) * M]
        blocks.append(block - jnp.mean(block, axis=1, keepdims=True))
    coeff = jnp.concatenate(blocks, axis=0)
    ch, cl = split2(coeff)
    scaled = modes[...] * (1.0 / ROOT)
    columns = [values[:, 2 + k].reshape(M, LEV) for k in range(2)]
    bh, bl = split2(jnp.concatenate(columns, axis=1))
    r = dot(ch, bh) + (dot(cl, bh) + dot(ch, bl))
    for k in range(2):
        total = columns[k]
        for a in range(L):
            total = total + scaled[a:a + 1] * r[a * M:(a + 1) * M, k * LEV:(k + 1) * LEV]
        out[:, k] = total.reshape(GROUPS, MD, LEV)


def call(kernel, outs, scratch, total, smem=0, name=None, cost=None):
    spaces = [pltpu.SMEM if n < smem else pltpu.VMEM for n in range(total)]
    return pl.pallas_call(
        kernel,
        out_shape=outs,
        in_specs=[pl.BlockSpec(memory_space=s) for s in spaces],
        out_specs=jax.tree.map(lambda _: pl.BlockSpec(memory_space=pltpu.VMEM), outs),
        scratch_shapes=scratch,
        compiler_params=pltpu.CompilerParams(vmem_limit_bytes=VMEM_LIMIT),
        name=name,
        cost_estimate=cost,
    )


def swap(x, axes):
    return lax.all_to_all(x, axes, split_axis=0, concat_axis=0, tiled=True)


def summed_copies(x, copies):
    total = jnp.sum(x, axis=0)
    return jnp.broadcast_to(total[None], (copies,) + total.shape)


def per_device(
    ensemble, neighbours, regime, norm_gain, up_weight, down_weight, vertical_modes,
    obs_col, obs_lev, obs_val, obs_err,
):
    shape = jax.ShapeDtypeStruct
    apart = [(n, n + 1) for n in range(1, 63, 2)]
    outer = lax.ppermute(ensemble, BANDS, apart + [(b, a) for a, b in apart])
    inner = lax.ppermute(ensemble, "core", [(0, 1), (1, 0)])
    lev = obs_lev.reshape(1, OBS)
    col = obs_col.reshape(1, OBS)
    val = obs_val.reshape(1, OBS)
    err = obs_err.reshape(1, OBS)
    one_hot, which, at_obs, place = call(
        prepare_kernel,
        [
            shape((LEV, OBS), BF), shape((C * MD, LEV), jnp.int32), shape((8, OBS), F32),
            shape((1, OBS), jnp.int32),
        ],
        [], 7, smem=1, name="prepare", cost=pl.CostEstimate(flops=1 << 33, bytes_accessed=1 << 20, transcendentals=0),
    )(
        regime, col, lev, val, err, vertical_modes,
        norm_gain.reshape(1, LEV),
    )
    values = call(
        forecast_kernel,
        shape((GROUPS, 4, MD, LEV), F32),
        [pltpu.VMEM((C + 2 * HALO, MD, LEV), F32), pltpu.VMEM((2, MD, HALO, LEV), F32)],
        10, smem=1, name="forecast",
    )(neighbours, ensemble, outer, inner, up_weight, down_weight, one_hot, which, at_obs, place)
    values = swap(values, "members")
    packed = call(
        gram_kernel,
        shape((8, PACKS, 8, M), F32),
        [pltpu.VMEM((M, OBS), F32)],
        2, name="gram",
    )(values, at_obs)
    packed = swap(packed, ("x", "core"))
    packed = swap(summed_copies(packed, 8), "z")
    mine = swap(summed_copies(packed, GROUPS), "members")
    other = lax.ppermute(mine, "core", [(0, 1), (1, 0)])
    size = L * M
    analysis = call(
        analysis_kernel,
        shape((GROUPS, 2, MD, LEV), F32),
        [
            pltpu.VMEM((PACKS, M, M), F32),
            pltpu.VMEM((L, M, M), F32),
            pltpu.VMEM((size, size), F32),
            pltpu.VMEM((2 * size + 2 * M, size), BF),
            pltpu.VMEM((size, size), BF),
        ],
        4, name="analysis",
    )(mine, other, values, vertical_modes)
    analysis = swap(analysis, "members")
    return analysis.transpose(2, 0, 1, 3).reshape(MD, C, LEV)


def solution(mesh):
    fine = Mesh(mesh.devices.reshape(8, 8, 4, 2), ("members",) + BANDS)
    in_specs = (
        P("members", BANDS, None),
        P(BANDS, None),
        P(BANDS),
        P(),
        P(),
        P(),
        P(),
        P(BANDS),
        P(BANDS),
        P(BANDS),
        P(BANDS),
    )
    out_specs = P("members", BANDS, None)
    return jax.shard_map(
        per_device, mesh=fine, in_specs=in_specs, out_specs=out_specs, check_vma=False
    )
```

```python
import functools
import math

import jax
import jax.numpy as jnp
from jax import lax
from jax.experimental import pallas as pl
from jax.experimental.pallas import tpu as pltpu
from jax.sharding import Mesh, PartitionSpec as P

E = 4
L = 4
NB = 4
HALO = 8
M = 128
LEV = 128
FF = 512
C = 16
MD = 16
OBS = 256
GROUPS = 8
PACKS = 7
PAIRS = [(a, b) for a in range(L) for b in range(a, L)]
ROOT = math.sqrt(L * M - 1)
BF = jnp.bfloat16
F32 = jnp.float32
VMEM_LIMIT = 40 * 1024 * 1024
BANDS = ("z", "x", "core")


def dot(a, b):
    return jnp.dot(a, b, preferred_element_type=F32)


def dot_nt(a, b):
    return lax.dot_general(a, b, (((1,), (1,)), ((), ())), preferred_element_type=F32)


def split2(a):
    high = a.astype(BF)
    return high, (a - high.astype(F32)).astype(BF)


def split3(a):
    high = a.astype(BF)
    rest = a - high.astype(F32)
    middle = rest.astype(BF)
    return high, middle, (rest - middle.astype(F32)).astype(BF)


def prepare_kernel(
    regime, col, lev, val, err, modes, gain,
    hot_out, regs_out, w_out, place_out,
):
    band = (lax.axis_index("z") * 4 + lax.axis_index("x")) * 2 + lax.axis_index("core")
    place_out[...] = col[...] - band * C
    for c in range(C):
        regs_out[c * MD:(c + 1) * MD, :] = jnp.full((MD, LEV), regime[c], jnp.int32)
    one_hot = (lax.broadcasted_iota(jnp.int32, (LEV, OBS), 0) == lev[...]).astype(F32).astype(BF)
    hot_out[...] = one_hot
    at_obs = None
    for part in split3(modes[...]):
        got = dot(part, one_hot)
        at_obs = got if at_obs is None else at_obs + got
    w_out[0:L, :] = at_obs
    w_out[L:L + 1, :] = val[...] / err[...]
    w_out[L + 1:L + 2, :] = err[...]
    w_out[L + 2:L + 3, 0:LEV] = gain[...]


def forecast_kernel(
    nb, ens, outer, inner, up, down, one_hot, which_ref, rows_in, place_in,
    v_out, wide, halves,
):
    core = lax.axis_index("core")
    band = (lax.axis_index("z") * 4 + lax.axis_index("x")) * 2 + core
    for c in range(C):
        wide[HALO + c] = ens[:, c, :]
    inner_at = (1 - core) * (HALO + C)
    outer_at = core * (HALO + C)
    halves[0] = inner[:, pl.ds(pl.multiple_of(core * HALO, HALO), HALO), :]
    halves[1] = outer[:, pl.ds(pl.multiple_of((1 - core) * HALO, HALO), HALO), :]
    for c in range(HALO):
        wide[inner_at + c] = halves[0, :, c, :]
        wide[outer_at + c] = halves[1, :, c, :]
    start = band * C - HALO
    rows = []
    for c in range(C):
        total = wide[nb[c, 0] - start]
        for k in range(1, NB):
            total = total + wide[nb[c, k] - start]
        own = wide[HALO + c]
        rows.append(own + 0.5 * (0.25 * total - own))
    flat = jnp.concatenate(rows, axis=0)
    inv_rms = lax.rsqrt(jnp.mean(flat * flat, axis=1, keepdims=True) + 1e-05)
    normed = (flat * inv_rms * rows_in[L + 2:L + 3, 0:LEV]).astype(BF)
    which = which_ref[...]
    which4 = jnp.concatenate([which] * (FF // LEV), axis=1)
    pre = dot(normed, up[0])
    for e in range(1, E):
        pre = jnp.where(which4 == e, dot(normed, up[e]), pre)
    hidden = pre / (1.0 + jnp.exp(-pre))
    tendency = None
    for e in range(E):
        part = dot(jnp.where(which4 == e, hidden, 0.0).astype(BF), down[e])
        tendency = part if tendency is None else tendency + part
    out = flat + tendency
    picked = None
    for part in split3(out):
        got = dot(part, one_hot[...])
        picked = got if picked is None else picked + got
    place = place_in[...]
    sampled = jnp.zeros((MD, OBS), F32)
    for c in range(C):
        sampled = sampled + jnp.where(place == c, picked[c * MD:(c + 1) * MD, :], 0.0)
    sampled = sampled / rows_in[L + 1:L + 2, :]
    for g in range(GROUPS):
        for k in range(2):
            v_out[g, k] = sampled[:, k * LEV:(k + 1) * LEV]
            v_out[g, 2 + k] = out[(2 * g + k) * MD:(2 * g + k + 1) * MD]


def gram_kernel(values, at_obs, packed, centred):
    group = lax.axis_index("members")
    raw = jnp.concatenate([values[:, k].reshape(M, LEV) for k in range(2)], axis=1)
    mean = jnp.sum(raw, axis=0, keepdims=True) * (1.0 / M)
    pert = raw - mean
    again = jnp.sum(pert, axis=0, keepdims=True) * (1.0 / M)
    pert = pert - again
    centred[...] = pert
    innovation = at_obs[L:L + 1, :] - (mean + again)
    own = centred[pl.ds(pl.multiple_of(group * MD, MD), MD), :]
    w = at_obs[...]
    weights = [w[a:a + 1] * w[b:b + 1] * (1.0 / (L * M - 1)) for a, b in PAIRS]
    weights += [w[a:a + 1] * (1.0 / ROOT) for a in range(L)]
    left = jnp.concatenate([own * f for f in weights], axis=0)
    right = jnp.concatenate(
        [pert, jnp.broadcast_to(innovation, (M, OBS))], axis=0
    )
    lh, ll = split2(left)
    rh, rl = split2(right)
    s = dot_nt(lh, rh) + (dot_nt(lh, rl) + dot_nt(ll, rh))
    row = lax.broadcasted_iota(jnp.int32, (MD, M), 0) + group * MD
    column = lax.broadcasted_iota(jnp.int32, (MD, M), 1)
    for t in range(PACKS):
        first = s[(2 * t) * MD:(2 * t + 1) * MD, :M]
        second = s[(2 * t + 1) * MD:(2 * t + 2) * MD, :M]
        if t < L:
            k = len(PAIRS) + t
            middle = s[k * MD:(k + 1) * MD, M:]
        else:
            middle = jnp.zeros((MD, M), F32)
        p = jnp.where(column > row, first, jnp.where(column < row, second, middle))
        for h in range(2):
            packed[2 * (t // 2) + h, t % 2] = p[8 * h:8 * h + 8]
    for h in range(2):
        packed[6 + h, 1] = jnp.zeros((8, M), F32)


def analysis_kernel(
    mine, other, values, modes, out,
    packed, crosses, zf, zh, fh,
):
    core = lax.axis_index("core")
    for g in range(GROUPS):
        for t in range(PACKS):
            at = pl.multiple_of(g * MD + core * 8, 8)
            packed[t, pl.ds(at, 8), :] = mine[4 * g + t // 2, t % 2]
            at = pl.multiple_of(g * MD + 8 - core * 8, 8)
            packed[t, pl.ds(at, 8), :] = other[4 * g + t // 2, t % 2]
    i = lax.broadcasted_iota(jnp.int32, (M, M), 0)
    j = lax.broadcasted_iota(jnp.int32, (M, M), 1)
    diagonal = i == j
    drives = []
    square = None
    for t in range(PACKS):
        p = packed[t]
        q = p.T
        if t < L:
            drives.append(jnp.sum(jnp.where(diagonal, p, 0.0), axis=0, keepdims=True))
        for side in range(2):
            keep = (i < j) if side == 0 else (i > j)
            s = jnp.where(diagonal, 0.0, jnp.where(keep, p, q))
            s = s - jnp.where(diagonal, jnp.sum(s, axis=0, keepdims=True), 0.0)
            k = 2 * t + side
            if k >= len(PAIRS):
                crosses[k - len(PAIRS)] = s
                continue
            a, b = PAIRS[k]
            if a == b:
                s = s + jnp.where(diagonal, 1.0, 0.0)
            zf[a * M:(a + 1) * M, b * M:(b + 1) * M] = s
            if a != b:
                zf[b * M:(b + 1) * M, a * M:(a + 1) * M] = s
            part = jnp.sum(s * s, axis=0, keepdims=True) * (1.0 if a == b else 2.0)
            square = part if square is None else square + part
    norm = jnp.sqrt(jnp.sum(square, axis=1, keepdims=True))
    inverse_norm = 1.0 / norm
    v = jnp.concatenate([drives[a] - 0.5 * crosses[a] for a in range(L)], axis=1)
    size = L * M
    z = zf[...] * inverse_norm
    for step in range(3):
        high, low = split2(z)
        zf[0:size] = z
        zh[0:size] = high
        zh[size:2 * size] = low
        vh, vl = split2(v)
        zh[2 * size:2 * size + M] = vh
        zh[2 * size + M:] = vl
        q = dot(zh[0:size], zh[0:size])
        fh[...] = (0.25 * q - 1.5 * zf[...]).astype(BF)
        if step == 2:
            new = dot(zh[2 * size:], fh[...])
            v = 2.25 * v + (new[:M] + new[M:])
            break
        new = dot(zh[...], fh[...])
        z = 2.25 * zf[...] + (new[0:size] + new[size:2 * size])
        v = 2.25 * v + (new[2 * size:2 * size + M] + new[2 * size + M:])
    for step in range(2):
        vh, vl = split2(v)
        got = dot(jnp.concatenate([vh, vl], axis=0), zh[0:size])
        got = got[:M] + (got[M:] + dot(vh, zh[size:2 * size]))
        th, tl = split2(got)
        new = dot(jnp.concatenate([th, tl], axis=0), fh[...])
        v = 1.5 * v - 0.5 * (2.25 * got + (new[:M] + new[M:]))
    v = v * inverse_norm
    blocks = []
    for a in range(L):
        block = v[:, a * M:(a + 1) * M]
        blocks.append(block - jnp.mean(block, axis=1, keepdims=True))
    coeff = jnp.concatenate(blocks, axis=0)
    ch, cl = split2(coeff)
    scaled = modes[...] * (1.0 / ROOT)
    columns = [values[:, 2 + k].reshape(M, LEV) for k in range(2)]
    bh, bl = split2(jnp.concatenate(columns, axis=1))
    r = dot(ch, bh) + (dot(cl, bh) + dot(ch, bl))
    for k in range(2):
        total = columns[k]
        for a in range(L):
            total = total + scaled[a:a + 1] * r[a * M:(a + 1) * M, k * LEV:(k + 1) * LEV]
        out[:, k] = total.reshape(GROUPS, MD, LEV)


def call(kernel, outs, scratch, total, smem=0, name=None, cost=None):
    spaces = [pltpu.SMEM if n < smem else pltpu.VMEM for n in range(total)]
    return pl.pallas_call(
        kernel,
        out_shape=outs,
        in_specs=[pl.BlockSpec(memory_space=s) for s in spaces],
        out_specs=jax.tree.map(lambda _: pl.BlockSpec(memory_space=pltpu.VMEM), outs),
        scratch_shapes=scratch,
        compiler_params=pltpu.CompilerParams(vmem_limit_bytes=VMEM_LIMIT),
        name=name,
        cost_estimate=cost,
    )


def swap(x, axes):
    return lax.all_to_all(x, axes, split_axis=0, concat_axis=0, tiled=True)


def summed_copies(x, copies):
    total = jnp.sum(x, axis=0)
    return jnp.broadcast_to(total[None], (copies,) + total.shape)


def per_device(
    ensemble, neighbours, regime, norm_gain, up_weight, down_weight, vertical_modes,
    obs_col, obs_lev, obs_val, obs_err,
):
    shape = jax.ShapeDtypeStruct
    apart = [(n, n + 1) for n in range(1, 63, 2)]
    outer = lax.ppermute(ensemble, BANDS, apart + [(b, a) for a, b in apart])
    inner = lax.ppermute(ensemble, "core", [(0, 1), (1, 0)])
    lev = obs_lev.reshape(1, OBS)
    col = obs_col.reshape(1, OBS)
    val = obs_val.reshape(1, OBS)
    err = obs_err.reshape(1, OBS)
    one_hot, which, at_obs, place = call(
        prepare_kernel,
        [
            shape((LEV, OBS), BF), shape((C * MD, LEV), jnp.int32), shape((8, OBS), F32),
            shape((1, OBS), jnp.int32),
        ],
        [], 7, smem=1, name="prepare", cost=pl.CostEstimate(flops=1 << 33, bytes_accessed=1 << 20, transcendentals=0),
    )(
        regime, col, lev, val, err, vertical_modes,
        norm_gain.reshape(1, LEV),
    )
    values = call(
        forecast_kernel,
        shape((GROUPS, 4, MD, LEV), F32),
        [pltpu.VMEM((C + 2 * HALO, MD, LEV), F32), pltpu.VMEM((2, MD, HALO, LEV), F32)],
        10, smem=1, name="forecast",
    )(neighbours, ensemble, outer, inner, up_weight, down_weight, one_hot, which, at_obs, place)
    values = swap(values, "members")
    packed = call(
        gram_kernel,
        shape((8, 2, 8, M), F32),
        [pltpu.VMEM((M, OBS), F32)],
        2, name="gram",
    )(values, at_obs)
    packed = swap(packed, ("x", "core"))
    packed = swap(summed_copies(packed, 8), "z")
    mine = swap(summed_copies(packed, 4 * GROUPS), ("members", "x"))
    other = lax.ppermute(mine, "core", [(0, 1), (1, 0)])
    size = L * M
    analysis = call(
        analysis_kernel,
        shape((GROUPS, 2, MD, LEV), F32),
        [
            pltpu.VMEM((PACKS, M, M), F32),
            pltpu.VMEM((L, M, M), F32),
            pltpu.VMEM((size, size), F32),
            pltpu.VMEM((2 * size + 2 * M, size), BF),
            pltpu.VMEM((size, size), BF),
        ],
        4, name="analysis",
    )(mine, other, values, vertical_modes)
    analysis = swap(analysis, "members")
    return analysis.transpose(2, 0, 1, 3).reshape(MD, C, LEV)


def solution(mesh):
    fine = Mesh(mesh.devices.reshape(8, 8, 4, 2), ("members",) + BANDS)
    in_specs = (
        P("members", BANDS, None),
        P(BANDS, None),
        P(BANDS),
        P(),
        P(),
        P(),
        P(),
        P(BANDS),
        P(BANDS),
        P(BANDS),
        P(BANDS),
    )
    out_specs = P("members", BANDS, None)
    return jax.shard_map(
        per_device, mesh=fine, in_specs=in_specs, out_specs=out_specs, check_vma=False
    )
```

```python
import functools
import math

import jax
import jax.numpy as jnp
from jax import lax
from jax.experimental import pallas as pl
from jax.experimental.pallas import tpu as pltpu
from jax.sharding import Mesh, PartitionSpec as P

E = 4
L = 4
NB = 4
HALO = 8
M = 128
LEV = 128
FF = 512
C = 16
MD = 16
OBS = 256
GROUPS = 8
PACKS = 7
PAIRS = [(a, b) for a in range(L) for b in range(a, L)]
ROOT = math.sqrt(L * M - 1)
BF = jnp.bfloat16
F32 = jnp.float32
VMEM_LIMIT = 40 * 1024 * 1024
BANDS = ("z", "x", "core")


def dot(a, b):
    return jnp.dot(a, b, preferred_element_type=F32)


def dot_nt(a, b):
    return lax.dot_general(a, b, (((1,), (1,)), ((), ())), preferred_element_type=F32)


def split2(a):
    high = a.astype(BF)
    return high, (a - high.astype(F32)).astype(BF)


def split3(a):
    high = a.astype(BF)
    rest = a - high.astype(F32)
    middle = rest.astype(BF)
    return high, middle, (rest - middle.astype(F32)).astype(BF)


def prepare_kernel(
    regime, col, lev, val, err, modes, gain,
    hot_out, regs_out, w_out, place_out,
):
    band = (lax.axis_index("z") * 4 + lax.axis_index("x")) * 2 + lax.axis_index("core")
    place_out[...] = col[...] - band * C
    for c in range(C):
        regs_out[c * MD:(c + 1) * MD, :] = jnp.full((MD, LEV), regime[c], jnp.int32)
    one_hot = (lax.broadcasted_iota(jnp.int32, (LEV, OBS), 0) == lev[...]).astype(F32).astype(BF)
    hot_out[...] = one_hot
    at_obs = None
    for part in split3(modes[...]):
        got = dot(part, one_hot)
        at_obs = got if at_obs is None else at_obs + got
    w_out[0:L, :] = at_obs
    w_out[L:L + 1, :] = val[...] / err[...]
    w_out[L + 1:L + 2, :] = err[...]
    w_out[L + 2:L + 3, 0:LEV] = gain[...]


def forecast_kernel(
    nb, ens, outer, inner, up, down, one_hot, which_ref, rows_in, place_in,
    v_out, wide, halves,
):
    core = lax.axis_index("core")
    band = (lax.axis_index("z") * 4 + lax.axis_index("x")) * 2 + core
    for c in range(C):
        wide[HALO + c] = ens[:, c, :]
    inner_at = (1 - core) * (HALO + C)
    outer_at = core * (HALO + C)
    halves[0] = inner[:, pl.ds(pl.multiple_of(core * HALO, HALO), HALO), :]
    halves[1] = outer[:, pl.ds(pl.multiple_of((1 - core) * HALO, HALO), HALO), :]
    for c in range(HALO):
        wide[inner_at + c] = halves[0, :, c, :]
        wide[outer_at + c] = halves[1, :, c, :]
    start = band * C - HALO
    rows = []
    for c in range(C):
        total = wide[nb[c, 0] - start]
        for k in range(1, NB):
            total = total + wide[nb[c, k] - start]
        own = wide[HALO + c]
        rows.append(own + 0.5 * (0.25 * total - own))
    flat = jnp.concatenate(rows, axis=0)
    inv_rms = lax.rsqrt(jnp.mean(flat * flat, axis=1, keepdims=True) + 1e-05)
    normed = (flat * inv_rms * rows_in[L + 2:L + 3, 0:LEV]).astype(BF)
    which = which_ref[...]
    which4 = jnp.concatenate([which] * (FF // LEV), axis=1)
    pre = dot(normed, up[0])
    for e in range(1, E):
        pre = jnp.where(which4 == e, dot(normed, up[e]), pre)
    hidden = pre / (1.0 + jnp.exp(-pre))
    tendency = None
    for e in range(E):
        part = dot(jnp.where(which4 == e, hidden, 0.0).astype(BF), down[e])
        tendency = part if tendency is None else tendency + part
    out = flat + tendency
    picked = None
    for part in split3(out):
        got = dot(part, one_hot[...])
        picked = got if picked is None else picked + got
    place = place_in[...]
    sampled = jnp.zeros((MD, OBS), F32)
    for c in range(C):
        sampled = sampled + jnp.where(place == c, picked[c * MD:(c + 1) * MD, :], 0.0)
    sampled = sampled / rows_in[L + 1:L + 2, :]
    for g in range(GROUPS):
        for k in range(2):
            v_out[g, k] = sampled[:, k * LEV:(k + 1) * LEV]
            v_out[g, 2 + k] = out[(2 * g + k) * MD:(2 * g + k + 1) * MD]


def gram_kernel(values, at_obs, packed, centred):
    group = lax.axis_index("members")
    raw = jnp.concatenate([values[:, k].reshape(M, LEV) for k in range(2)], axis=1)
    mean = jnp.sum(raw, axis=0, keepdims=True) * (1.0 / M)
    pert = raw - mean
    again = jnp.sum(pert, axis=0, keepdims=True) * (1.0 / M)
    pert = pert - again
    centred[...] = pert
    innovation = at_obs[L:L + 1, :] - (mean + again)
    own = centred[pl.ds(pl.multiple_of(group * MD, MD), MD), :]
    w = at_obs[...]
    weights = [w[a:a + 1] * w[b:b + 1] * (1.0 / (L * M - 1)) for a, b in PAIRS]
    weights += [w[a:a + 1] * (1.0 / ROOT) for a in range(L)]
    left = jnp.concatenate([own * f for f in weights], axis=0)
    right = jnp.concatenate(
        [pert, jnp.broadcast_to(innovation, (M, OBS))], axis=0
    )
    lh, ll = split2(left)
    rh, rl = split2(right)
    s = dot_nt(lh, rh) + (dot_nt(lh, rl) + dot_nt(ll, rh))
    row = lax.broadcasted_iota(jnp.int32, (MD, M), 0) + group * MD
    column = lax.broadcasted_iota(jnp.int32, (MD, M), 1)
    for t in range(PACKS):
        first = s[(2 * t) * MD:(2 * t + 1) * MD, :M]
        second = s[(2 * t + 1) * MD:(2 * t + 2) * MD, :M]
        if t < L:
            k = len(PAIRS) + t
            middle = s[k * MD:(k + 1) * MD, M:]
        else:
            middle = jnp.zeros((MD, M), F32)
        p = jnp.where(column > row, first, jnp.where(column < row, second, middle))
        for h in range(2):
            packed[2 * (t // 2) + h, t % 2] = p[8 * h:8 * h + 8]
    for h in range(2):
        packed[6 + h, 1] = jnp.zeros((8, M), F32)


def analysis_kernel(
    mine, other, values, modes, out,
    packed, crosses, zf, zh, fh,
):
    core = lax.axis_index("core")
    for g in range(GROUPS):
        for t in range(PACKS):
            at = pl.multiple_of(g * MD + core * 8, 8)
            packed[t, pl.ds(at, 8), :] = mine[GROUPS * (t // 2) + g, t % 2]
            at = pl.multiple_of(g * MD + 8 - core * 8, 8)
            packed[t, pl.ds(at, 8), :] = other[GROUPS * (t // 2) + g, t % 2]
    i = lax.broadcasted_iota(jnp.int32, (M, M), 0)
    j = lax.broadcasted_iota(jnp.int32, (M, M), 1)
    diagonal = i == j
    drives = []
    square = None
    for t in range(PACKS):
        p = packed[t]
        q = p.T
        if t < L:
            drives.append(jnp.sum(jnp.where(diagonal, p, 0.0), axis=0, keepdims=True))
        for side in range(2):
            keep = (i < j) if side == 0 else (i > j)
            s = jnp.where(diagonal, 0.0, jnp.where(keep, p, q))
            s = s - jnp.where(diagonal, jnp.sum(s, axis=0, keepdims=True), 0.0)
            k = 2 * t + side
            if k >= len(PAIRS):
                crosses[k - len(PAIRS)] = s
                continue
            a, b = PAIRS[k]
            if a == b:
                s = s + jnp.where(diagonal, 1.0, 0.0)
            zf[a * M:(a + 1) * M, b * M:(b + 1) * M] = s
            if a != b:
                zf[b * M:(b + 1) * M, a * M:(a + 1) * M] = s
            part = jnp.sum(s * s, axis=0, keepdims=True) * (1.0 if a == b else 2.0)
            square = part if square is None else square + part
    norm = jnp.sqrt(jnp.sum(square, axis=1, keepdims=True))
    inverse_norm = 1.0 / norm
    v = jnp.concatenate([drives[a] - 0.5 * crosses[a] for a in range(L)], axis=1)
    size = L * M
    z = zf[...] * inverse_norm
    for step in range(3):
        if step == 0:
            high, low = split2(z)
            zf[...] = z
            zh[0:size] = high
            zh[size:2 * size] = low
        vh, vl = split2(v)
        zh[2 * size:2 * size + M] = vh
        zh[2 * size + M:] = vl
        for r in range(0, size, M):
            to = r + M
            q = dot(zh[r:to], zh[0:size])
            fh[r:to] = (0.25 * q - 1.5 * zf[r:to]).astype(BF)
        if step == 2:
            new = dot(zh[2 * size:], fh[...])
            v = 2.25 * v + (new[:M] + new[M:])
            break
        for r in range(0, size, M):
            to = r + M
            both = jnp.concatenate([zh[r:to], zh[size + r:size + to]], axis=0)
            new = dot(both, fh[...])
            piece = 2.25 * zf[r:to] + (new[:M] + new[M:])
            zf[r:to] = piece
            high, low = split2(piece)
            zh[r:to] = high
            zh[size + r:size + to] = low
        new = dot(zh[2 * size:], fh[...])
        v = 2.25 * v + (new[:M] + new[M:])
    for step in range(2):
        vh, vl = split2(v)
        got = dot(jnp.concatenate([vh, vl], axis=0), zh[0:size])
        got = got[:M] + (got[M:] + dot(vh, zh[size:2 * size]))
        th, tl = split2(got)
        new = dot(jnp.concatenate([th, tl], axis=0), fh[...])
        v = 1.5 * v - 0.5 * (2.25 * got + (new[:M] + new[M:]))
    v = v * inverse_norm
    blocks = []
    for a in range(L):
        block = v[:, a * M:(a + 1) * M]
        blocks.append(block - jnp.mean(block, axis=1, keepdims=True))
    coeff = jnp.concatenate(blocks, axis=0)
    ch, cl = split2(coeff)
    scaled = modes[...] * (1.0 / ROOT)
    columns = [values[:, 2 + k].reshape(M, LEV) for k in range(2)]
    bh, bl = split2(jnp.concatenate(columns, axis=1))
    r = dot(ch, bh) + (dot(cl, bh) + dot(ch, bl))
    for k in range(2):
        total = columns[k]
        for a in range(L):
            total = total + scaled[a:a + 1] * r[a * M:(a + 1) * M, k * LEV:(k + 1) * LEV]
        out[:, k] = total.reshape(GROUPS, MD, LEV)


def call(kernel, outs, scratch, total, smem=0, name=None, cost=None):
    spaces = [pltpu.SMEM if n < smem else pltpu.VMEM for n in range(total)]
    return pl.pallas_call(
        kernel,
        out_shape=outs,
        in_specs=[pl.BlockSpec(memory_space=s) for s in spaces],
        out_specs=jax.tree.map(lambda _: pl.BlockSpec(memory_space=pltpu.VMEM), outs),
        scratch_shapes=scratch,
        compiler_params=pltpu.CompilerParams(vmem_limit_bytes=VMEM_LIMIT),
        name=name,
        cost_estimate=cost,
    )


def swap(x, axes):
    return lax.all_to_all(x, axes, split_axis=0, concat_axis=0, tiled=True)


def summed_copies(x, copies):
    total = jnp.sum(x, axis=0)
    return jnp.broadcast_to(total[None], (copies,) + total.shape)


def per_device(
    ensemble, neighbours, regime, norm_gain, up_weight, down_weight, vertical_modes,
    obs_col, obs_lev, obs_val, obs_err,
):
    shape = jax.ShapeDtypeStruct
    apart = [(n, n + 1) for n in range(1, 63, 2)]
    outer = lax.ppermute(ensemble, BANDS, apart + [(b, a) for a, b in apart])
    inner = lax.ppermute(ensemble, "core", [(0, 1), (1, 0)])
    lev = obs_lev.reshape(1, OBS)
    col = obs_col.reshape(1, OBS)
    val = obs_val.reshape(1, OBS)
    err = obs_err.reshape(1, OBS)
    one_hot, which, at_obs, place = call(
        prepare_kernel,
        [
            shape((LEV, OBS), BF), shape((C * MD, LEV), jnp.int32), shape((8, OBS), F32),
            shape((1, OBS), jnp.int32),
        ],
        [], 7, smem=1, name="prepare", cost=pl.CostEstimate(flops=1 << 33, bytes_accessed=1 << 20, transcendentals=0),
    )(
        regime, col, lev, val, err, vertical_modes,
        norm_gain.reshape(1, LEV),
    )
    values = call(
        forecast_kernel,
        shape((GROUPS, 4, MD, LEV), F32),
        [pltpu.VMEM((C + 2 * HALO, MD, LEV), F32), pltpu.VMEM((2, MD, HALO, LEV), F32)],
        10, smem=1, name="forecast",
    )(neighbours, ensemble, outer, inner, up_weight, down_weight, one_hot, which, at_obs, place)
    values = swap(values, "members")
    packed = call(
        gram_kernel,
        shape((8, 2, 8, M), F32),
        [pltpu.VMEM((M, OBS), F32)],
        2, name="gram",
    )(values, at_obs)
    packed = swap(packed, ("x", "core"))
    packed = swap(summed_copies(packed, 8), "z")
    mine = swap(summed_copies(packed, 4 * GROUPS), ("x", "members"))
    other = lax.ppermute(mine, "core", [(0, 1), (1, 0)])
    size = L * M
    analysis = call(
        analysis_kernel,
        shape((GROUPS, 2, MD, LEV), F32),
        [
            pltpu.VMEM((PACKS, M, M), F32),
            pltpu.VMEM((L, M, M), F32),
            pltpu.VMEM((size, size), F32),
            pltpu.VMEM((2 * size + 2 * M, size), BF),
            pltpu.VMEM((size, size), BF),
        ],
        4, name="analysis",
    )(mine, other, values, vertical_modes)
    analysis = swap(analysis, "members")
    return analysis.transpose(2, 0, 1, 3).reshape(MD, C, LEV)


def solution(mesh):
    fine = Mesh(mesh.devices.reshape(8, 8, 4, 2), ("members",) + BANDS)
    in_specs = (
        P("members", BANDS, None),
        P(BANDS, None),
        P(BANDS),
        P(),
        P(),
        P(),
        P(),
        P(BANDS),
        P(BANDS),
        P(BANDS),
        P(BANDS),
    )
    out_specs = P("members", BANDS, None)
    return jax.shard_map(
        per_device, mesh=fine, in_specs=in_specs, out_specs=out_specs, check_vma=False
    )
```

```python
import functools
import math

import jax
import jax.numpy as jnp
from jax import lax
from jax.experimental import pallas as pl
from jax.experimental.pallas import tpu as pltpu
from jax.sharding import Mesh, PartitionSpec as P

E = 4
L = 4
NB = 4
HALO = 8
M = 128
LEV = 128
FF = 512
C = 16
MD = 16
OBS = 256
GROUPS = 8
PACKS = 7
PAIRS = [(a, b) for a in range(L) for b in range(a, L)]
ROOT = math.sqrt(L * M - 1)
BF = jnp.bfloat16
F32 = jnp.float32
VMEM_LIMIT = 40 * 1024 * 1024
BANDS = ("z", "x", "core")


def dot(a, b):
    return jnp.dot(a, b, preferred_element_type=F32)


def dot_nt(a, b):
    return lax.dot_general(a, b, (((1,), (1,)), ((), ())), preferred_element_type=F32)


def split2(a):
    high = a.astype(BF)
    return high, (a - high.astype(F32)).astype(BF)


def split3(a):
    high = a.astype(BF)
    rest = a - high.astype(F32)
    middle = rest.astype(BF)
    return high, middle, (rest - middle.astype(F32)).astype(BF)


def prepare_kernel(
    regime, col, lev, val, err, modes, gain,
    hot_out, regs_out, w_out, place_out,
):
    band = (lax.axis_index("z") * 4 + lax.axis_index("x")) * 2 + lax.axis_index("core")
    place_out[...] = col[...] - band * C
    for c in range(C):
        regs_out[c * MD:(c + 1) * MD, :] = jnp.full((MD, LEV), regime[c], jnp.int32)
    one_hot = (lax.broadcasted_iota(jnp.int32, (LEV, OBS), 0) == lev[...]).astype(F32).astype(BF)
    hot_out[...] = one_hot
    at_obs = None
    for part in split3(modes[...]):
        got = dot(part, one_hot)
        at_obs = got if at_obs is None else at_obs + got
    w_out[0:L, :] = at_obs
    w_out[L:L + 1, :] = val[...] / err[...]
    w_out[L + 1:L + 2, :] = err[...]
    w_out[L + 2:L + 3, 0:LEV] = gain[...]


def forecast_kernel(
    nb, ens, outer, inner, up, down, one_hot, which_ref, rows_in, place_in,
    v_out, wide, halves,
):
    core = lax.axis_index("core")
    band = (lax.axis_index("z") * 4 + lax.axis_index("x")) * 2 + core
    for c in range(C):
        wide[HALO + c] = ens[:, c, :]
    inner_at = (1 - core) * (HALO + C)
    outer_at = core * (HALO + C)
    halves[0] = inner[:, pl.ds(pl.multiple_of(core * HALO, HALO), HALO), :]
    halves[1] = outer[:, pl.ds(pl.multiple_of((1 - core) * HALO, HALO), HALO), :]
    for c in range(HALO):
        wide[inner_at + c] = halves[0, :, c, :]
        wide[outer_at + c] = halves[1, :, c, :]
    start = band * C - HALO
    rows = []
    for c in range(C):
        total = wide[nb[c, 0] - start]
        for k in range(1, NB):
            total = total + wide[nb[c, k] - start]
        own = wide[HALO + c]
        rows.append(own + 0.5 * (0.25 * total - own))
    flat = jnp.concatenate(rows, axis=0)
    inv_rms = lax.rsqrt(jnp.mean(flat * flat, axis=1, keepdims=True) + 1e-05)
    normed = (flat * inv_rms * rows_in[L + 2:L + 3, 0:LEV]).astype(BF)
    which = which_ref[...]
    which4 = jnp.concatenate([which] * (FF // LEV), axis=1)
    pre = dot(normed, up[0])
    for e in range(1, E):
        pre = jnp.where(which4 == e, dot(normed, up[e]), pre)
    hidden = pre / (1.0 + jnp.exp(-pre))
    tendency = None
    for e in range(E):
        part = dot(jnp.where(which4 == e, hidden, 0.0).astype(BF), down[e])
        tendency = part if tendency is None else tendency + part
    out = flat + tendency
    picked = None
    for part in split3(out):
        got = dot(part, one_hot[...])
        picked = got if picked is None else picked + got
    place = place_in[...]
    sampled = jnp.zeros((MD, OBS), F32)
    for c in range(C):
        sampled = sampled + jnp.where(place == c, picked[c * MD:(c + 1) * MD, :], 0.0)
    sampled = sampled / rows_in[L + 1:L + 2, :]
    for g in range(GROUPS):
        for k in range(2):
            v_out[g, k] = sampled[:, k * LEV:(k + 1) * LEV]
            v_out[g, 2 + k] = out[(2 * g + k) * MD:(2 * g + k + 1) * MD]


def gram_kernel(values, at_obs, packed, centred):
    group = lax.axis_index("members")
    raw = jnp.concatenate([values[:, k].reshape(M, LEV) for k in range(2)], axis=1)
    mean = jnp.sum(raw, axis=0, keepdims=True) * (1.0 / M)
    pert = raw - mean
    again = jnp.sum(pert, axis=0, keepdims=True) * (1.0 / M)
    pert = pert - again
    centred[...] = pert
    innovation = at_obs[L:L + 1, :] - (mean + again)
    own = centred[pl.ds(pl.multiple_of(group * MD, MD), MD), :]
    w = at_obs[...]
    weights = [w[a:a + 1] * w[b:b + 1] * (1.0 / (L * M - 1)) for a, b in PAIRS]
    weights += [w[a:a + 1] * (1.0 / ROOT) for a in range(L)]
    left = jnp.concatenate([own * f for f in weights], axis=0)
    right = jnp.concatenate(
        [pert, jnp.broadcast_to(innovation, (M, OBS))], axis=0
    )
    lh, ll = split2(left)
    rh, rl = split2(right)
    s = dot_nt(lh, rh) + (dot_nt(lh, rl) + dot_nt(ll, rh))
    row = lax.broadcasted_iota(jnp.int32, (MD, M), 0) + group * MD
    column = lax.broadcasted_iota(jnp.int32, (MD, M), 1)
    for t in range(PACKS):
        first = s[(2 * t) * MD:(2 * t + 1) * MD, :M]
        second = s[(2 * t + 1) * MD:(2 * t + 2) * MD, :M]
        if t < L:
            k = len(PAIRS) + t
            middle = s[k * MD:(k + 1) * MD, M:]
        else:
            middle = jnp.zeros((MD, M), F32)
        p = jnp.where(column > row, first, jnp.where(column < row, second, middle))
        for h in range(2):
            packed[4 * h + t // 2, t % 2] = p[8 * h:8 * h + 8]
    for h in range(2):
        packed[4 * h + 3, 1] = jnp.zeros((8, M), F32)


def analysis_kernel(
    mine, other, values, modes, out,
    packed, crosses, zf, zh, fh,
):
    core = lax.axis_index("core")
    for g in range(GROUPS):
        for t in range(PACKS):
            at = pl.multiple_of(g * MD + core * 8, 8)
            packed[t, pl.ds(at, 8), :] = mine[GROUPS * (t // 2) + g, t % 2]
            at = pl.multiple_of(g * MD + 8 - core * 8, 8)
            packed[t, pl.ds(at, 8), :] = other[GROUPS * (t // 2) + g, t % 2]
    i = lax.broadcasted_iota(jnp.int32, (M, M), 0)
    j = lax.broadcasted_iota(jnp.int32, (M, M), 1)
    diagonal = i == j
    drives = []
    square = None
    for t in range(PACKS):
        p = packed[t]
        q = p.T
        if t < L:
            drives.append(jnp.sum(jnp.where(diagonal, p, 0.0), axis=0, keepdims=True))
        for side in range(2):
            keep = (i < j) if side == 0 else (i > j)
            s = jnp.where(diagonal, 0.0, jnp.where(keep, p, q))
            s = s - jnp.where(diagonal, jnp.sum(s, axis=0, keepdims=True), 0.0)
            k = 2 * t + side
            if k >= len(PAIRS):
                crosses[k - len(PAIRS)] = s
                continue
            a, b = PAIRS[k]
            if a == b:
                s = s + jnp.where(diagonal, 1.0, 0.0)
            zf[a * M:(a + 1) * M, b * M:(b + 1) * M] = s
            if a != b:
                zf[b * M:(b + 1) * M, a * M:(a + 1) * M] = s
            part = jnp.sum(s * s, axis=0, keepdims=True) * (1.0 if a == b else 2.0)
            square = part if square is None else square + part
    norm = jnp.sqrt(jnp.sum(square, axis=1, keepdims=True))
    inverse_norm = 1.0 / norm
    v = jnp.concatenate([drives[a] - 0.5 * crosses[a] for a in range(L)], axis=1)
    size = L * M
    z = zf[...] * inverse_norm
    for step in range(3):
        if step == 0:
            high, low = split2(z)
            zf[...] = z
            zh[0:size] = high
            zh[size:2 * size] = low
        vh, vl = split2(v)
        zh[2 * size:2 * size + M] = vh
        zh[2 * size + M:] = vl
        for r in range(0, size, M):
            to = r + M
            q = dot(zh[r:to], zh[0:size])
            fh[r:to] = (0.25 * q - 1.5 * zf[r:to]).astype(BF)
        if step == 2:
            new = dot(zh[2 * size:], fh[...])
            v = 2.25 * v + (new[:M] + new[M:])
            break
        for r in range(0, size, M):
            to = r + M
            both = jnp.concatenate([zh[r:to], zh[size + r:size + to]], axis=0)
            new = dot(both, fh[...])
            piece = 2.25 * zf[r:to] + (new[:M] + new[M:])
            zf[r:to] = piece
            high, low = split2(piece)
            zh[r:to] = high
            zh[size + r:size + to] = low
        new = dot(zh[2 * size:], fh[...])
        v = 2.25 * v + (new[:M] + new[M:])
    for step in range(2):
        vh, vl = split2(v)
        got = dot(jnp.concatenate([vh, vl], axis=0), zh[0:size])
        got = got[:M] + (got[M:] + dot(vh, zh[size:2 * size]))
        th, tl = split2(got)
        new = dot(jnp.concatenate([th, tl], axis=0), fh[...])
        v = 1.5 * v - 0.5 * (2.25 * got + (new[:M] + new[M:]))
    v = v * inverse_norm
    blocks = []
    for a in range(L):
        block = v[:, a * M:(a + 1) * M]
        blocks.append(block - jnp.mean(block, axis=1, keepdims=True))
    coeff = jnp.concatenate(blocks, axis=0)
    ch, cl = split2(coeff)
    scaled = modes[...] * (1.0 / ROOT)
    columns = [values[:, 2 + k].reshape(M, LEV) for k in range(2)]
    bh, bl = split2(jnp.concatenate(columns, axis=1))
    r = dot(ch, bh) + (dot(cl, bh) + dot(ch, bl))
    for k in range(2):
        total = columns[k]
        for a in range(L):
            total = total + scaled[a:a + 1] * r[a * M:(a + 1) * M, k * LEV:(k + 1) * LEV]
        out[:, k] = total.reshape(GROUPS, MD, LEV)


def call(kernel, outs, scratch, total, smem=0, name=None, cost=None):
    spaces = [pltpu.SMEM if n < smem else pltpu.VMEM for n in range(total)]
    return pl.pallas_call(
        kernel,
        out_shape=outs,
        in_specs=[pl.BlockSpec(memory_space=s) for s in spaces],
        out_specs=jax.tree.map(lambda _: pl.BlockSpec(memory_space=pltpu.VMEM), outs),
        scratch_shapes=scratch,
        compiler_params=pltpu.CompilerParams(vmem_limit_bytes=VMEM_LIMIT),
        name=name,
        cost_estimate=cost,
    )


def swap(x, axes):
    return lax.all_to_all(x, axes, split_axis=0, concat_axis=0, tiled=True)


def summed_copies(x, copies):
    total = jnp.sum(x, axis=0)
    return jnp.broadcast_to(total[None], (copies,) + total.shape)


def per_device(
    ensemble, neighbours, regime, norm_gain, up_weight, down_weight, vertical_modes,
    obs_col, obs_lev, obs_val, obs_err,
):
    shape = jax.ShapeDtypeStruct
    apart = [(n, n + 1) for n in range(1, 63, 2)]
    outer = lax.ppermute(ensemble, BANDS, apart + [(b, a) for a, b in apart])
    inner = lax.ppermute(ensemble, "core", [(0, 1), (1, 0)])
    lev = obs_lev.reshape(1, OBS)
    col = obs_col.reshape(1, OBS)
    val = obs_val.reshape(1, OBS)
    err = obs_err.reshape(1, OBS)
    one_hot, which, at_obs, place = call(
        prepare_kernel,
        [
            shape((LEV, OBS), BF), shape((C * MD, LEV), jnp.int32), shape((8, OBS), F32),
            shape((1, OBS), jnp.int32),
        ],
        [], 7, smem=1, name="prepare", cost=pl.CostEstimate(flops=1 << 33, bytes_accessed=1 << 20, transcendentals=0),
    )(
        regime, col, lev, val, err, vertical_modes,
        norm_gain.reshape(1, LEV),
    )
    values = call(
        forecast_kernel,
        shape((GROUPS, 4, MD, LEV), F32),
        [pltpu.VMEM((C + 2 * HALO, MD, LEV), F32), pltpu.VMEM((2, MD, HALO, LEV), F32)],
        10, smem=1, name="forecast",
    )(neighbours, ensemble, outer, inner, up_weight, down_weight, one_hot, which, at_obs, place)
    values = swap(values, "members")
    packed = call(
        gram_kernel,
        shape((8, 2, 8, M), F32),
        [pltpu.VMEM((M, OBS), F32)],
        2, name="gram",
    )(values, at_obs)
    packed = swap(packed, ("core", "x"))
    packed = swap(summed_copies(packed, 8), "z")
    mine = swap(summed_copies(packed, 4 * GROUPS), ("x", "members"))
    other = lax.ppermute(mine, "core", [(0, 1), (1, 0)])
    size = L * M
    analysis = call(
        analysis_kernel,
        shape((GROUPS, 2, MD, LEV), F32),
        [
            pltpu.VMEM((PACKS, M, M), F32),
            pltpu.VMEM((L, M, M), F32),
            pltpu.VMEM((size, size), F32),
            pltpu.VMEM((2 * size + 2 * M, size), BF),
            pltpu.VMEM((size, size), BF),
        ],
        4, name="analysis",
    )(mine, other, values, vertical_modes)
    analysis = swap(analysis, "members")
    return analysis.transpose(2, 0, 1, 3).reshape(MD, C, LEV)


def solution(mesh):
    fine = Mesh(mesh.devices.reshape(8, 8, 4, 2), ("members",) + BANDS)
    in_specs = (
        P("members", BANDS, None),
        P(BANDS, None),
        P(BANDS),
        P(),
        P(),
        P(),
        P(),
        P(BANDS),
        P(BANDS),
        P(BANDS),
        P(BANDS),
    )
    out_specs = P("members", BANDS, None)
    return jax.shard_map(
        per_device, mesh=fine, in_specs=in_specs, out_specs=out_specs, check_vma=False
    )
```

```python
import functools
import math

import jax
import jax.numpy as jnp
from jax import lax
from jax.experimental import pallas as pl
from jax.experimental.pallas import tpu as pltpu
from jax.sharding import Mesh, PartitionSpec as P

E = 4
L = 4
NB = 4
HALO = 8
M = 128
LEV = 128
FF = 512
C = 16
MD = 16
OBS = 256
GROUPS = 8
PACKS = 7
PAIRS = [(a, b) for a in range(L) for b in range(a, L)]
ROOT = math.sqrt(L * M - 1)
BF = jnp.bfloat16
F32 = jnp.float32
VMEM_LIMIT = 40 * 1024 * 1024
BANDS = ("z", "x", "core")


def dot(a, b):
    return jnp.dot(a, b, preferred_element_type=F32)


def dot_nt(a, b):
    return lax.dot_general(a, b, (((1,), (1,)), ((), ())), preferred_element_type=F32)


def split2(a):
    high = a.astype(BF)
    return high, (a - high.astype(F32)).astype(BF)


def split3(a):
    high = a.astype(BF)
    rest = a - high.astype(F32)
    middle = rest.astype(BF)
    return high, middle, (rest - middle.astype(F32)).astype(BF)


def prepare_kernel(
    regime, col, lev, val, err, modes, gain,
    hot_out, regs_out, w_out, place_out,
):
    band = (lax.axis_index("z") * 4 + lax.axis_index("x")) * 2 + lax.axis_index("core")
    place_out[...] = col[...] - band * C
    for c in range(C):
        regs_out[c * MD:(c + 1) * MD, :] = jnp.full((MD, LEV), regime[c], jnp.int32)
    one_hot = (lax.broadcasted_iota(jnp.int32, (LEV, OBS), 0) == lev[...]).astype(F32).astype(BF)
    hot_out[...] = one_hot
    at_obs = None
    for part in split3(modes[...]):
        got = dot(part, one_hot)
        at_obs = got if at_obs is None else at_obs + got
    w_out[0:L, :] = at_obs
    w_out[L:L + 1, :] = val[...] / err[...]
    w_out[L + 1:L + 2, :] = err[...]
    w_out[L + 2:L + 3, 0:LEV] = gain[...]


def forecast_kernel(
    nb, ens, outer, inner, up, down, one_hot, which_ref, rows_in, place_in,
    v_out, wide, halves,
):
    core = lax.axis_index("core")
    band = (lax.axis_index("z") * 4 + lax.axis_index("x")) * 2 + core
    for c in range(C):
        wide[HALO + c] = ens[:, c, :]
    inner_at = (1 - core) * (HALO + C)
    outer_at = core * (HALO + C)
    halves[0] = inner[:, pl.ds(pl.multiple_of(core * HALO, HALO), HALO), :]
    halves[1] = outer[:, pl.ds(pl.multiple_of((1 - core) * HALO, HALO), HALO), :]
    for c in range(HALO):
        wide[inner_at + c] = halves[0, :, c, :]
        wide[outer_at + c] = halves[1, :, c, :]
    start = band * C - HALO
    rows = []
    for c in range(C):
        total = wide[nb[c, 0] - start]
        for k in range(1, NB):
            total = total + wide[nb[c, k] - start]
        own = wide[HALO + c]
        rows.append(own + 0.5 * (0.25 * total - own))
    flat = jnp.concatenate(rows, axis=0)
    inv_rms = lax.rsqrt(jnp.mean(flat * flat, axis=1, keepdims=True) + 1e-05)
    normed = (flat * inv_rms * rows_in[L + 2:L + 3, 0:LEV]).astype(BF)
    pieces = []
    for r in range(0, C * MD, M):
        rows_here = normed[r:r + M]
        which4 = jnp.concatenate([which_ref[r:r + M]] * (FF // LEV), axis=1)
        pre = dot(rows_here, up[0])
        for e in range(1, E):
            pre = jnp.where(which4 == e, dot(rows_here, up[e]), pre)
        hidden = pre / (1.0 + jnp.exp(-pre))
        piece = None
        for e in range(E):
            part = dot(jnp.where(which4 == e, hidden, 0.0).astype(BF), down[e])
            piece = part if piece is None else piece + part
        pieces.append(piece)
    tendency = jnp.concatenate(pieces, axis=0)
    out = flat + tendency
    picked = None
    for part in split3(out):
        got = dot(part, one_hot[...])
        picked = got if picked is None else picked + got
    place = place_in[...]
    sampled = jnp.zeros((MD, OBS), F32)
    for c in range(C):
        sampled = sampled + jnp.where(place == c, picked[c * MD:(c + 1) * MD, :], 0.0)
    sampled = sampled / rows_in[L + 1:L + 2, :]
    for g in range(GROUPS):
        for k in range(2):
            v_out[g, k] = sampled[:, k * LEV:(k + 1) * LEV]
            v_out[g, 2 + k] = out[(2 * g + k) * MD:(2 * g + k + 1) * MD]


def gram_kernel(values, at_obs, packed, centred):
    group = lax.axis_index("members")
    raw = jnp.concatenate([values[:, k].reshape(M, LEV) for k in range(2)], axis=1)
    mean = jnp.sum(raw, axis=0, keepdims=True) * (1.0 / M)
    pert = raw - mean
    again = jnp.sum(pert, axis=0, keepdims=True) * (1.0 / M)
    pert = pert - again
    centred[...] = pert
    innovation = at_obs[L:L + 1, :] - (mean + again)
    own = centred[pl.ds(pl.multiple_of(group * MD, MD), MD), :]
    w = at_obs[...]
    weights = [w[a:a + 1] * w[b:b + 1] * (1.0 / (L * M - 1)) for a, b in PAIRS]
    weights += [w[a:a + 1] * (1.0 / ROOT) for a in range(L)]
    left = jnp.concatenate([own * f for f in weights], axis=0)
    right = jnp.concatenate(
        [pert, jnp.broadcast_to(innovation, (M, OBS))], axis=0
    )
    lh, ll = split2(left)
    rh, rl = split2(right)
    s = dot_nt(lh, rh) + (dot_nt(lh, rl) + dot_nt(ll, rh))
    row = lax.broadcasted_iota(jnp.int32, (MD, M), 0) + group * MD
    column = lax.broadcasted_iota(jnp.int32, (MD, M), 1)
    for t in range(PACKS):
        first = s[(2 * t) * MD:(2 * t + 1) * MD, :M]
        second = s[(2 * t + 1) * MD:(2 * t + 2) * MD, :M]
        if t < L:
            k = len(PAIRS) + t
            middle = s[k * MD:(k + 1) * MD, M:]
        else:
            middle = jnp.zeros((MD, M), F32)
        p = jnp.where(column > row, first, jnp.where(column < row, second, middle))
        for h in range(2):
            packed[2 * (t // 2) + h, t % 2] = p[8 * h:8 * h + 8]
    for h in range(2):
        packed[6 + h, 1] = jnp.zeros((8, M), F32)


def analysis_kernel(
    mine, other, values, modes, out,
    packed, crosses, zf, zh, fh,
):
    core = lax.axis_index("core")
    for g in range(GROUPS):
        for t in range(PACKS):
            at = pl.multiple_of(g * MD + core * 8, 8)
            packed[t, pl.ds(at, 8), :] = mine[GROUPS * (t // 2) + g, t % 2]
            at = pl.multiple_of(g * MD + 8 - core * 8, 8)
            packed[t, pl.ds(at, 8), :] = other[GROUPS * (t // 2) + g, t % 2]
    i = lax.broadcasted_iota(jnp.int32, (M, M), 0)
    j = lax.broadcasted_iota(jnp.int32, (M, M), 1)
    diagonal = i == j
    drives = []
    square = None
    for t in range(PACKS):
        p = packed[t]
        q = p.T
        if t < L:
            drives.append(jnp.sum(jnp.where(diagonal, p, 0.0), axis=0, keepdims=True))
        for side in range(2):
            keep = (i < j) if side == 0 else (i > j)
            s = jnp.where(diagonal, 0.0, jnp.where(keep, p, q))
            s = s - jnp.where(diagonal, jnp.sum(s, axis=0, keepdims=True), 0.0)
            k = 2 * t + side
            if k >= len(PAIRS):
                crosses[k - len(PAIRS)] = s
                continue
            a, b = PAIRS[k]
            if a == b:
                s = s + jnp.where(diagonal, 1.0, 0.0)
            zf[a * M:(a + 1) * M, b * M:(b + 1) * M] = s
            if a != b:
                zf[b * M:(b + 1) * M, a * M:(a + 1) * M] = s
            part = jnp.sum(s * s, axis=0, keepdims=True) * (1.0 if a == b else 2.0)
            square = part if square is None else square + part
    norm = jnp.sqrt(jnp.sum(square, axis=1, keepdims=True))
    inverse_norm = 1.0 / norm
    v = jnp.concatenate([drives[a] - 0.5 * crosses[a] for a in range(L)], axis=1)
    size = L * M
    z = zf[...] * inverse_norm
    for step in range(3):
        if step == 0:
            high, low = split2(z)
            zf[...] = z
            zh[0:size] = high
            zh[size:2 * size] = low
        vh, vl = split2(v)
        zh[2 * size:2 * size + M] = vh
        zh[2 * size + M:] = vl
        for r in range(0, size, M):
            to = r + M
            q = dot(zh[r:to], zh[0:size])
            fh[r:to] = (0.25 * q - 1.5 * zf[r:to]).astype(BF)
        if step == 2:
            new = dot(zh[2 * size:], fh[...])
            v = 2.25 * v + (new[:M] + new[M:])
            break
        for r in range(0, size, M):
            to = r + M
            both = jnp.concatenate([zh[r:to], zh[size + r:size + to]], axis=0)
            new = dot(both, fh[...])
            piece = 2.25 * zf[r:to] + (new[:M] + new[M:])
            zf[r:to] = piece
            high, low = split2(piece)
            zh[r:to] = high
            zh[size + r:size + to] = low
        new = dot(zh[2 * size:], fh[...])
        v = 2.25 * v + (new[:M] + new[M:])
    for step in range(2):
        vh, vl = split2(v)
        got = dot(jnp.concatenate([vh, vl], axis=0), zh[0:size])
        got = got[:M] + (got[M:] + dot(vh, zh[size:2 * size]))
        th, tl = split2(got)
        new = dot(jnp.concatenate([th, tl], axis=0), fh[...])
        v = 1.5 * v - 0.5 * (2.25 * got + (new[:M] + new[M:]))
    v = v * inverse_norm
    blocks = []
    for a in range(L):
        block = v[:, a * M:(a + 1) * M]
        blocks.append(block - jnp.mean(block, axis=1, keepdims=True))
    coeff = jnp.concatenate(blocks, axis=0)
    ch, cl = split2(coeff)
    scaled = modes[...] * (1.0 / ROOT)
    columns = [values[:, 2 + k].reshape(M, LEV) for k in range(2)]
    bh, bl = split2(jnp.concatenate(columns, axis=1))
    r = dot(ch, bh) + (dot(cl, bh) + dot(ch, bl))
    for k in range(2):
        total = columns[k]
        for a in range(L):
            total = total + scaled[a:a + 1] * r[a * M:(a + 1) * M, k * LEV:(k + 1) * LEV]
        out[:, k] = total.reshape(GROUPS, MD, LEV)


def call(kernel, outs, scratch, total, smem=0, name=None, cost=None):
    spaces = [pltpu.SMEM if n < smem else pltpu.VMEM for n in range(total)]
    return pl.pallas_call(
        kernel,
        out_shape=outs,
        in_specs=[pl.BlockSpec(memory_space=s) for s in spaces],
        out_specs=jax.tree.map(lambda _: pl.BlockSpec(memory_space=pltpu.VMEM), outs),
        scratch_shapes=scratch,
        compiler_params=pltpu.CompilerParams(vmem_limit_bytes=VMEM_LIMIT),
        name=name,
        cost_estimate=cost,
    )


def swap(x, axes):
    return lax.all_to_all(x, axes, split_axis=0, concat_axis=0, tiled=True)


def summed_copies(x, copies):
    total = jnp.sum(x, axis=0)
    return jnp.broadcast_to(total[None], (copies,) + total.shape)


def per_device(
    ensemble, neighbours, regime, norm_gain, up_weight, down_weight, vertical_modes,
    obs_col, obs_lev, obs_val, obs_err,
):
    shape = jax.ShapeDtypeStruct
    apart = [(n, n + 1) for n in range(1, 63, 2)]
    outer = lax.ppermute(ensemble, BANDS, apart + [(b, a) for a, b in apart])
    inner = lax.ppermute(ensemble, "core", [(0, 1), (1, 0)])
    lev = obs_lev.reshape(1, OBS)
    col = obs_col.reshape(1, OBS)
    val = obs_val.reshape(1, OBS)
    err = obs_err.reshape(1, OBS)
    one_hot, which, at_obs, place = call(
        prepare_kernel,
        [
            shape((LEV, OBS), BF), shape((C * MD, LEV), jnp.int32), shape((8, OBS), F32),
            shape((1, OBS), jnp.int32),
        ],
        [], 7, smem=1, name="prepare", cost=pl.CostEstimate(flops=1 << 33, bytes_accessed=1 << 20, transcendentals=0),
    )(
        regime, col, lev, val, err, vertical_modes,
        norm_gain.reshape(1, LEV),
    )
    values = call(
        forecast_kernel,
        shape((GROUPS, 4, MD, LEV), F32),
        [pltpu.VMEM((C + 2 * HALO, MD, LEV), F32), pltpu.VMEM((2, MD, HALO, LEV), F32)],
        10, smem=1, name="forecast",
    )(neighbours, ensemble, outer, inner, up_weight, down_weight, one_hot, which, at_obs, place)
    values = swap(values, "members")
    packed = call(
        gram_kernel,
        shape((8, 2, 8, M), F32),
        [pltpu.VMEM((M, OBS), F32)],
        2, name="gram",
    )(values, at_obs)
    packed = swap(packed, ("x", "core"))
    packed = swap(summed_copies(packed, 8), "z")
    mine = swap(summed_copies(packed, 4 * GROUPS), ("x", "members"))
    other = lax.ppermute(mine, "core", [(0, 1), (1, 0)])
    size = L * M
    analysis = call(
        analysis_kernel,
        shape((GROUPS, 2, MD, LEV), F32),
        [
            pltpu.VMEM((PACKS, M, M), F32),
            pltpu.VMEM((L, M, M), F32),
            pltpu.VMEM((size, size), F32),
            pltpu.VMEM((2 * size + 2 * M, size), BF),
            pltpu.VMEM((size, size), BF),
        ],
        4, name="analysis",
    )(mine, other, values, vertical_modes)
    analysis = swap(analysis, "members")
    return analysis.transpose(2, 0, 1, 3).reshape(MD, C, LEV)


def solution(mesh):
    fine = Mesh(mesh.devices.reshape(8, 8, 4, 2), ("members",) + BANDS)
    in_specs = (
        P("members", BANDS, None),
        P(BANDS, None),
        P(BANDS),
        P(),
        P(),
        P(),
        P(),
        P(BANDS),
        P(BANDS),
        P(BANDS),
        P(BANDS),
    )
    out_specs = P("members", BANDS, None)
    return jax.shard_map(
        per_device, mesh=fine, in_specs=in_specs, out_specs=out_specs, check_vma=False
    )
```
